512 devices in a mesh: expert: 8 (over z_lo, core), row: 4 (over x), col: 16 (over y, z_hi).
Axes of the slice: x: 4, y: 4, z: 16 (z_hi: 4, z_lo: 4; z = z_hi * 4 + z_lo), core: 2. Of those that a mesh axis runs over, the one named last changes fastest.
Arguments:
- tokens: bfloat16 [8, 1024, 4096], P('expert', 'col', 'row'), may hold values from -6 to 6
- routes: int32 [8, 2], replicated, may hold values from 0 to 7, all different within a row; in each aligned block of 8 rows (0 to 7, 8 to 15, ...) at most 2 rows name the same one
- route_gates: float32 [8, 2], replicated, may hold values from 0.1 to 1
- w_in: bfloat16 [8, 4096, 2, 7168], P('expert', 'row', None, 'col'), may hold values from -0.09375 to 0.09375
- w_down: bfloat16 [8, 7168, 4096], P('expert', 'col', 'row'), may hold values from -0.0625 to 0.0625
Outputs:
- mixed: bfloat16 [8, 1024, 4096], P('expert', 'col', 'row')
The draws below stay inside these ranges and needn't reach their ends.
Inputs may be any that keep to these rules, and one draw needn't show every extreme that they name: `routes`: each row names two different experts; every expert is named by exactly 2 rows.
All inputs are finite; a program needn't handle non-finite values.
Results may differ from the reference program's by a relative error of at most 0.03.
Values may be sent and summed in bfloat16 or wider, within the bound.
No kernel may reach another device: no remote copies, remote signals or barrier semaphores. Data moves between devices by JAX's collectives and lax.ppermute only.
A program may use at most 128 MiB of HBM per device.

```python
import math
import jax
import jax.numpy as jnp
import numpy as np
from jax import lax

D = 4096
FF = 7168
LEN = 1024
EXPERTS = 8
SEQS = 8
CAP = 2
FF_PARTS = 16


def level_of(key, shape, cuts, smallest, top_value):
    def one(dim, parts):
        heights = jax.random.uniform(jax.random.fold_in(jax.random.fold_in(key, 6), dim), (parts,), jnp.float32, smallest / len(cuts), top_value / len(cuts))
        return jnp.repeat(jnp.exp(heights), shape[dim] // parts).reshape((-1,) + (1,) * (len(shape) - dim - 1))

    loudness = one(*cuts[0])
    for cut in cuts[1:]:
        loudness = loudness * one(*cut)
    return loudness


def routed_block(rng, own, number, rows, amount, top, most, slope):
    order = jax.random.permutation(rng, amount)
    crowded, ordinary = portions_of(amount, rows * top, most, slope, True), portions_of(amount, rows * top, most, slope, False)
    places = jnp.arange(amount)

    def named(tallies, offset_by):
        used = int((tallies > 0).sum())
        fixed = max(1, used // 4)
        passed = fixed + (places - fixed + offset_by * (used - fixed)) % max(1, amount - fixed)
        return jnp.zeros((amount,), jnp.int32).at[order[jnp.where(places < fixed, places, passed)]].set(jnp.asarray(tallies, jnp.int32))

    tallies = jnp.where(number % 4 == 0, named(crowded, number // 4), named(ordinary, number - number // 4 - 1))
    mixed = jax.random.permutation(jax.random.fold_in(own, 3), amount)
    donor, sink = mixed[0:amount // 2 * 2:2], mixed[1:amount // 2 * 2:2]
    slack = jnp.minimum(tallies[donor] - 1, most - tallies[sink]) // 2
    slack = jnp.where((donor == order[0]) | (sink == order[0]) | (tallies[sink] == 0), 0, jnp.maximum(slack, 0))
    passed = jax.random.randint(jax.random.fold_in(own, 4), (amount // 2,), 0, 1 << 20) % (slack + 1)
    tallies = tallies.at[donor].add(-passed).at[sink].add(passed)
    items = jnp.searchsorted(jnp.cumsum(tallies), jnp.arange(rows * top), side="right").astype(jnp.int32)
    listing = items.reshape(top, rows).T
    listing = listing[jax.random.permutation(jax.random.fold_in(own, 1), rows)]
    offset_by = jax.random.randint(jax.random.fold_in(own, 2), (rows, 1), 0, top)
    return jnp.take_along_axis(listing, (jnp.arange(top)[None, :] + offset_by) % top, axis=1)


def portions_of(count, total, reach, skew, full):
    loads = [(1 << 20) // math.isqrt(grade ** skew) + 1 for grade in range(1, count + 1)]
    largest = reach if full else min(reach, max(-(-total // count), total * loads[0] // sum(loads)))
    least = 1 if total - largest >= count - 1 else 0
    holding, spare = [largest] + [least] * (count - 1), total - largest - least * (count - 1)
    while spare > 0:
        candidates = [i for i in range(1, count) if holding[i] < largest] or [i for i in range(1, count) if holding[i] < reach]
        mass, left = sum([loads[i] for i in candidates]), spare
        for i in candidates:
            extra = min(reach - holding[i], max(1, left * loads[i] // mass), spare)
            holding[i] = holding[i] + extra
            spare = spare - extra
    return np.array(holding)


def bell_draw(rng, dims, spread, most, shards=(), held_as=jnp.bfloat16):
    level = level_of(rng, dims, shards, -0.22, 0.18) if shards else 1.0
    drawn = jax.random.normal(rng, dims, jnp.float32) * spread * level
    return jnp.minimum(jnp.maximum(drawn, -most), most).astype(held_as)


def setup_inputs(seed: int = 0) -> dict:
    keys = jax.random.split(jax.random.key(seed), 6)
    tokens = bell_draw(keys[0], (SEQS, LEN, D), 1.0, 6.0, ((0, 8), (1, 16), (2, 4)))
    routes_keys = jax.random.split(jax.random.fold_in(keys[1], 1), SEQS // SEQS)
    routes_turns = jax.random.permutation(jax.random.fold_in(keys[1], 3), SEQS // SEQS)
    routes = jax.vmap(lambda own, number: routed_block(jax.random.fold_in(keys[1], 2), own, number, SEQS, EXPERTS, 2, CAP, 2))(routes_keys, routes_turns).reshape((SEQS, 2))
    route_gates = jnp.clip(jax.random.uniform(keys[2], (SEQS, 2), jnp.float32, 0.1, 1.0), 0.1, 1.0)
    w_in = bell_draw(keys[3], (EXPERTS, D, 2, FF), D ** -0.5, 0.09375, ((0, 8), (1, 4), (3, 16)))
    w_down = bell_draw(keys[4], (EXPERTS, FF, D), FF ** -0.5, 0.0625, ((0, 8), (1, 16), (2, 4)))
    return dict(tokens=tokens, routes=routes, route_gates=route_gates, w_in=w_in, w_down=w_down)


def reference(tokens, routes, route_gates, w_in, w_down):
    labels = jnp.arange(EXPERTS, dtype=jnp.int32)
    hit = jnp.sum((routes[:, :, None] == labels[None, None, :]).astype(jnp.int32), axis=1)
    slot = jnp.cumsum(hit, axis=0) - hit
    places = jnp.arange(CAP, dtype=jnp.int32)
    tokens_wide = tokens.astype(jnp.float32)

    def one_expert(index):
        taken = lax.dynamic_index_in_dim(hit, index, 1, keepdims=False)
        where = lax.dynamic_index_in_dim(slot, index, 1, keepdims=False)
        select = ((where[:, None] == places[None, :]) & (taken[:, None] == 1)).astype(jnp.float32)
        packed = jnp.einsum("sk,spd->pkd", select, tokens_wide).astype(jnp.bfloat16)
        rows = packed.reshape(LEN * CAP, D)
        w_both = lax.dynamic_index_in_dim(w_in, index, 0, keepdims=False).reshape(D, 2 * FF)
        gate_up = jnp.dot(rows, w_both, preferred_element_type=jnp.float32)
        hidden = (jax.nn.silu(gate_up[:, :FF]) * gate_up[:, FF:]).astype(jnp.bfloat16)
        w_out = lax.dynamic_index_in_dim(w_down, index, 0, keepdims=False)
        blocks = hidden.reshape(LEN * CAP, FF_PARTS, FF // FF_PARTS).astype(jnp.float32)
        w_blocks = w_out.reshape(FF_PARTS, FF // FF_PARTS, D).astype(jnp.float32)
        partials = jnp.einsum("tcf,cfd->ctd", blocks, w_blocks)
        rounded = lax.optimization_barrier(partials.astype(jnp.bfloat16))
        total = jnp.sum(rounded.astype(jnp.float32), axis=0).astype(jnp.bfloat16)
        return total.reshape(LEN, CAP, D)

    results = lax.map(one_expert, jnp.arange(EXPERTS, dtype=jnp.int32))
    mixed = jnp.zeros((SEQS, LEN, D), jnp.float32)
    for column in range(2):
        chosen = routes[:, column]
        chosen_slot = jnp.take_along_axis(slot, routes[:, column:column + 1], axis=1)[:, 0]
        picked = results[chosen, :, chosen_slot, :]
        mixed = mixed + route_gates[:, column][:, None, None] * picked.astype(jnp.float32)
    return mixed.astype(jnp.bfloat16)
```

```python
import jax
import jax.numpy as jnp
from jax import lax
from jax.sharding import Mesh, PartitionSpec as P


def shift(a, axis, by):
    n = lax.axis_size(axis)
    return lax.ppermute(a, axis, [(i, (i + by) % n) for i in range(n)])


def ring_gather(a, axis):
    half = a.shape[0] // 2
    below = shift(a, axis, 1)
    above = shift(a, axis, -1)
    low = shift(below[:half], axis, 1)
    high = shift(above[half:], axis, -1)
    return a, above, jnp.concatenate([low, high]), below


def ring_scatter(parts, axis):
    me, above, far, below = parts
    half = far.shape[0] // 2
    wide = jnp.float32
    up = shift(far[:half].astype(jnp.bfloat16), axis, 1)
    down = shift(far[half:].astype(jnp.bfloat16), axis, -1)
    above = jnp.concatenate([above[:half].astype(wide) + up.astype(wide), above[half:].astype(wide)])
    below = jnp.concatenate([below[:half].astype(wide), below[half:].astype(wide) + down.astype(wide)])
    up = shift(above.astype(jnp.bfloat16), axis, 1)
    down = shift(below.astype(jnp.bfloat16), axis, -1)
    return me.astype(wide) + up.astype(wide) + down.astype(wide)


def on_device(tokens, routes, route_gates, w_in, w_down):
    wide = jnp.float32
    core = lax.axis_index("core")
    expert = lax.axis_index("zlo") * 2 + core
    matches = routes[:, :, None] == jnp.arange(8, dtype=jnp.int32)[None, None, :]
    hit = jnp.sum(matches.astype(jnp.int32), axis=1)
    slot = jnp.cumsum(hit, axis=0) - hit
    weight = jnp.sum(route_gates[:, :, None] * matches.astype(wide), axis=1)
    taken = lax.dynamic_index_in_dim(hit, expert, 1, keepdims=False)
    place = lax.dynamic_index_in_dim(slot, expert, 1, keepdims=False)
    gates = lax.dynamic_index_in_dim(weight, expert, 1, keepdims=False)
    names = jnp.arange(8, dtype=jnp.int32)
    chosen = [(taken == 1) & (place == k) for k in range(2)]
    seqs = [jnp.sum(jnp.where(c, names, 0)) for c in chosen]
    scales = [jnp.sum(jnp.where(c, gates, 0.0)) for c in chosen]

    w_t = jnp.transpose(w_in[0], (1, 2, 0)).reshape(896, 1024)
    w_parts = ring_gather(w_t, "y")
    v_parts = ring_gather(w_down[0], "y")

    mine = lax.all_to_all(
        jnp.broadcast_to(tokens, (4, 64, 1024)), "zlo", split_axis=0, concat_axis=0, tiled=True
    )
    other = shift(mine, "core", 1)
    rows = []
    for s in seqs:
        a = lax.dynamic_index_in_dim(mine, s // 2, 0, keepdims=False)
        b = lax.dynamic_index_in_dim(other, s // 2, 0, keepdims=False)
        rows.append(jnp.where(s % 2 == core, a, b))
    rows = jnp.concatenate(ring_gather(jnp.concatenate(rows), "zhi"))

    w_all = jnp.concatenate([w[:448] for w in w_parts] + [w[448:] for w in w_parts])
    sums = lax.dot_general(
        rows, w_all, (((1,), (1,)), ((), ())), preferred_element_type=wide
    ).astype(jnp.bfloat16)
    parts = lax.all_to_all(sums.reshape(4, 128, 3584), "x", split_axis=0, concat_axis=0, tiled=True)
    total = jnp.sum(parts.astype(wide), axis=0)
    hidden = (jax.nn.silu(total[:, :1792]) * total[:, 1792:]).astype(jnp.bfloat16)
    hidden = lax.all_to_all(
        jnp.broadcast_to(hidden[None], (4, 128, 1792)), "x", split_axis=0, concat_axis=0, tiled=True
    ).reshape(512, 1792)

    v_all = jnp.concatenate(v_parts)
    out = jnp.dot(hidden, v_all, preferred_element_type=wide).astype(jnp.bfloat16).reshape(4, 128, 1024)
    result = ring_scatter((out[0], out[1], out[2], out[3]), "zhi").reshape(2, 64, 1024)

    ids = jnp.arange(4, dtype=jnp.int32)[:, None, None]
    def toward(parity):
        return sum(
            jnp.where((s // 2 == ids) & (s % 2 == parity), scale * result[k][None], 0.0)
            for k, (s, scale) in enumerate(zip(seqs, scales))
        )
    got = shift(toward(1 - core).astype(jnp.bfloat16), "core", 1)
    going = (toward(core) + got.astype(wide)).astype(jnp.bfloat16)
    back = lax.all_to_all(going, "zlo", split_axis=0, concat_axis=0, tiled=True)
    return jnp.sum(back.astype(wide), axis=0, keepdims=True).astype(jnp.bfloat16)


def solution(mesh):
    fine = Mesh(mesh.devices.reshape(4, 2, 4, 4, 4), ("zlo", "core", "x", "y", "zhi"))
    seqs, pos = ("zlo", "core"), ("y", "zhi")
    return jax.shard_map(
        on_device,
        mesh=fine,
        in_specs=(
            P(seqs, pos, "x"),
            P(),
            P(),
            P(seqs, "x", None, pos),
            P(seqs, pos, "x"),
        ),
        out_specs=P(seqs, pos, "x"),
        check_vma=False,
    )
```

```python
import jax
import jax.numpy as jnp
from jax import lax
from jax.experimental import pallas as pl
from jax.experimental.pallas import tpu as pltpu
from jax.sharding import Mesh, PartitionSpec as P

wide = jnp.float32
half = jnp.bfloat16


def shift(a, axis, by):
    n = lax.axis_size(axis)
    return lax.ppermute(a, axis, [(i, (i + by) % n) for i in range(n)])


def swap(a, axis):
    return lax.all_to_all(a, axis, split_axis=0, concat_axis=0, tiled=True)


def gate_up(pieces, w_all, after=None):
    n = len(pieces)
    rows = 128 * n

    def kernel(*refs):
        w_ref, out_ref, x_ref = refs[n], refs[-2], refs[-1]

        @pl.when(pl.program_id(0) == 0)
        def _():
            for j in range(4):
                for i in range(n):
                    x_ref[pl.ds(32 * (j * n + i), 32), :] = refs[i][pl.ds(32 * j, 32), :]

        w = w_ref[...].reshape(896, 1024)
        out = lax.dot_general(x_ref[...], w, (((1,), (1,)), ((), ())), preferred_element_type=wide)
        out_ref[...] = out.astype(half).reshape(4, 32 * n, 896)

    whole = pl.BlockSpec((128, 1024), lambda i: (0, 0))
    w_spec = pl.BlockSpec((2, 1, 448, 1024), lambda i: (i % 2, i // 2, 0, 0))
    extra = [] if after is None else [after]
    return pl.pallas_call(
        kernel,
        grid=(4,),
        in_specs=[whole] * n + [w_spec] + [pl.BlockSpec(memory_space=pl.ANY)] * len(extra),
        out_specs=pl.BlockSpec((4, 32 * n, 896), lambda i: (0, 0, i)),
        out_shape=jax.ShapeDtypeStruct((4, 32 * n, 3584), half),
        scratch_shapes=[pltpu.VMEM((rows, 1024), half)],
        compiler_params=pltpu.CompilerParams(vmem_limit_bytes=24 * 2**20),
        cost_estimate=pl.CostEstimate(
            flops=2 * rows * 1024 * 3584, bytes_accessed=3584 * 2048 + rows * 9216, transcendentals=0
        ),
    )(*pieces, w_all, *extra)


def activate(sums, cuts):
    rows = sums.shape[1]

    def kernel(gate_ref, up_ref, *outs):
        gate = jnp.sum(gate_ref[...].astype(wide), axis=0)
        up = jnp.sum(up_ref[...].astype(wide), axis=0)
        hidden = (gate / (1.0 + jnp.exp(-gate)) * up).astype(half)
        at = 0
        for cut, out in zip(cuts, outs):
            for j in range(4):
                out[j] = hidden[at : at + cut]
            at += cut

    return pl.pallas_call(
        kernel,
        grid=(2,),
        in_specs=[
            pl.BlockSpec((4, rows, 896), lambda i: (0, 0, i)),
            pl.BlockSpec((4, rows, 896), lambda i: (0, 0, i + 2)),
        ],
        out_specs=[pl.BlockSpec((4, c, 896), lambda i: (0, 0, i)) for c in cuts],
        out_shape=[jax.ShapeDtypeStruct((4, c, 1792), half) for c in cuts],
        compiler_params=pltpu.CompilerParams(vmem_limit_bytes=24 * 2**20),
        cost_estimate=pl.CostEstimate(
            flops=rows * 1792 * 12, bytes_accessed=rows * 3584 * 12, transcendentals=rows * 1792
        ),
    )(sums, sums)


def on_device(tokens, routes, route_gates, w_in, w_down):
    core = lax.axis_index("core")
    expert = lax.axis_index("zlo") * 2 + core
    w_t = jnp.transpose(w_in[0], (1, 2, 0)).reshape(896, 1024)
    w_all = lax.all_gather(w_t, "y", axis=0, tiled=True).reshape(4, 2, 448, 1024)

    matches = routes[:, :, None] == jnp.arange(8, dtype=jnp.int32)[None, None, :]
    hit = jnp.sum(matches.astype(jnp.int32), axis=1)
    slot = jnp.cumsum(hit, axis=0) - hit
    weight = jnp.sum(route_gates[:, :, None] * matches.astype(wide), axis=1)
    taken = lax.dynamic_index_in_dim(hit, expert, 1, keepdims=False)
    place = lax.dynamic_index_in_dim(slot, expert, 1, keepdims=False)
    gates = lax.dynamic_index_in_dim(weight, expert, 1, keepdims=False)
    names = jnp.arange(8, dtype=jnp.int32)
    chosen = [(taken == 1) & (place == k) for k in range(2)]
    owner = [jnp.sum(jnp.where(c, names >> 1, 0)) for c in chosen]
    side = [jnp.sum(jnp.where(c, names & 1, 0)) for c in chosen]
    scales = [jnp.sum(jnp.where(c, gates, 0.0)) for c in chosen]

    mine = swap(jnp.broadcast_to(tokens, (4, 64, 1024)), "zlo")
    other = shift(mine, "core", 1)
    rows = []
    for z, c in zip(owner, side):
        a = lax.dynamic_index_in_dim(mine, z, 0, keepdims=False)
        b = lax.dynamic_index_in_dim(other, z, 0, keepdims=False)
        rows.append(jnp.where(c == core, a, b))
    rows = jnp.concatenate(rows)

    above = shift(rows, "zhi", -1)
    below = shift(rows, "zhi", 1)
    low = shift(below[:64], "zhi", 1)
    high = shift(above[64:], "zhi", -1)
    far = jnp.concatenate([low, high])
    v_all = lax.all_gather(w_down[0], "y", axis=0, tiled=True)

    def down(hidden):
        return jnp.dot(hidden.reshape(-1, 1792), v_all, preferred_element_type=wide)

    sums = swap(gate_up([far, above, below], w_all), "x")
    far_h, near_h = activate(sums, (32, 64))
    far_h = swap(far_h, "x")
    far_out = down(far_h).astype(half)
    up1 = shift(far_out[:64], "zhi", 1)
    down1 = shift(far_out[64:], "zhi", -1)
    near_h = swap(near_h, "x")
    near_out = down(near_h).reshape(4, 2, 32, 1024)
    above_out = near_out[:, 0].reshape(128, 1024)
    below_out = near_out[:, 1].reshape(128, 1024)
    above_out = jnp.concatenate([above_out[:64] + up1.astype(wide), above_out[64:]]).astype(half)
    below_out = jnp.concatenate([below_out[:64], below_out[64:] + down1.astype(wide)]).astype(half)
    up2 = shift(above_out, "zhi", 1)
    down2 = shift(below_out, "zhi", -1)

    own = swap(gate_up([rows], w_all, near_h), "x")
    (own_h,) = activate(own, (32,))
    own_h = swap(own_h, "x")
    result = (down(own_h) + up2.astype(wide) + down2.astype(wide)).reshape(2, 64, 1024)

    ids = jnp.arange(4, dtype=jnp.int32)[:, None, None]

    def toward(parity):
        return sum(
            jnp.where((owner[k] == ids) & (side[k] == parity), scales[k] * result[k][None], 0.0)
            for k in range(2)
        )

    got = shift(toward(1 - core).astype(half), "core", 1)
    going = (toward(core) + got.astype(wide)).astype(half)
    back = swap(going, "zlo")
    return jnp.sum(back.astype(wide), axis=0, keepdims=True).astype(half)


def solution(mesh):
    fine = Mesh(mesh.devices.reshape(4, 2, 4, 4, 4), ("zlo", "core", "x", "y", "zhi"))
    seqs, pos = ("zlo", "core"), ("y", "zhi")
    return jax.shard_map(
        on_device,
        mesh=fine,
        in_specs=(
            P(seqs, pos, "x"),
            P(),
            P(),
            P(seqs, "x", None, pos),
            P(seqs, pos, "x"),
        ),
        out_specs=P(seqs, pos, "x"),
        check_vma=False,
    )
```

```python
import jax
import jax.numpy as jnp
from jax import lax
from jax.experimental import pallas as pl
from jax.experimental.pallas import tpu as pltpu
from jax.sharding import Mesh, PartitionSpec as P

wide = jnp.float32
half = jnp.bfloat16
LIMIT = 60 * 2**20
ANY = pl.BlockSpec(memory_space=pl.ANY)


def shift(a, axis, by):
    n = lax.axis_size(axis)
    return lax.ppermute(a, axis, [(i, (i + by) % n) for i in range(n)])


def onward(a, axis):
    n = lax.axis_size(axis)
    return lax.ppermute(
        a, ("core", axis), [(c * n + i, c * n + (i + 1 - 2 * c) % n) for c in range(2) for i in range(n)]
    )


def swap(a, axis):
    return lax.all_to_all(a, axis, split_axis=0, concat_axis=0, tiled=True)


def hold(a, after):
    def kernel(a_ref, after_ref, out_ref, sem):
        copy = pltpu.make_async_copy(a_ref, out_ref, sem)
        copy.start()
        copy.wait()

    return pl.pallas_call(
        kernel,
        in_specs=[ANY, ANY],
        out_specs=ANY,
        out_shape=jax.ShapeDtypeStruct(a.shape, a.dtype),
        scratch_shapes=[pltpu.SemaphoreType.DMA],
        compiler_params=pltpu.CompilerParams(vmem_limit_bytes=LIMIT),
        cost_estimate=pl.CostEstimate(flops=0, bytes_accessed=4 * a.size, transcendentals=0),
    )(a, after)


def gate_up(pieces, weights, after=None):
    n = len(pieces)
    rows = 128 * n

    def kernel(*refs):
        w_refs, out_ref, x_ref = refs[n : n + 4], refs[-2], refs[-1]

        @pl.when(pl.program_id(0) == 0)
        def _():
            for j in range(4):
                for i in range(n):
                    x_ref[pl.ds(32 * (j * n + i), 32), :] = refs[i][pl.ds(32 * j, 32), :]

        for p in range(2):
            w = jnp.concatenate([w_refs[2 * p][...], w_refs[2 * p + 1][...]])
            out = lax.dot_general(x_ref[...], w, (((1,), (1,)), ((), ())), preferred_element_type=wide)
            out_ref[:, :, pl.ds(896 * p, 896)] = out.astype(half).reshape(4, 32 * n, 896)

    whole = pl.BlockSpec((128, 1024), lambda i: (0, 0))
    extra = [] if after is None else [after]
    return pl.pallas_call(
        kernel,
        grid=(2,),
        in_specs=[whole] * n + [pl.BlockSpec((448, 1024), lambda i: (i, 0))] * 4 + [ANY] * len(extra),
        out_specs=pl.BlockSpec((4, 32 * n, 1792), lambda i: (0, 0, i)),
        out_shape=jax.ShapeDtypeStruct((4, 32 * n, 3584), half),
        scratch_shapes=[pltpu.VMEM((rows, 1024), half)],
        compiler_params=pltpu.CompilerParams(vmem_limit_bytes=LIMIT),
        cost_estimate=pl.CostEstimate(
            flops=2 * rows * 1024 * 3584, bytes_accessed=3584 * 2048 + rows * 9216, transcendentals=0
        ),
    )(*pieces, *weights, *extra)


def activate(sums, *after):
    rows = sums.shape[1]

    def kernel(gate_ref, up_ref, *refs):
        out_ref = refs[-1]
        gate = jnp.sum(gate_ref[...].astype(wide), axis=0)
        up = jnp.sum(up_ref[...].astype(wide), axis=0)
        hidden = (gate / (1.0 + jnp.exp(-gate)) * up).astype(half)
        for j in range(4):
            out_ref[j] = hidden

    return pl.pallas_call(
        kernel,
        grid=(2,),
        in_specs=[
            pl.BlockSpec((4, rows, 896), lambda i: (0, 0, i)),
            pl.BlockSpec((4, rows, 896), lambda i: (0, 0, i + 2)),
        ]
        + [ANY] * len(after),
        out_specs=pl.BlockSpec((4, rows, 896), lambda i: (0, 0, i)),
        out_shape=jax.ShapeDtypeStruct((4, rows, 1792), half),
        compiler_params=pltpu.CompilerParams(vmem_limit_bytes=LIMIT),
        cost_estimate=pl.CostEstimate(
            flops=rows * 1792 * 12, bytes_accessed=rows * 3584 * 12, transcendentals=rows * 1792
        ),
    )(sums, sums, *after)


def down(hidden, weights, types):
    n = len(types)

    def kernel(*refs):
        hidden_ref, v_refs, outs = refs[0], refs[1:5], refs[5:]
        v = jnp.concatenate([ref[...] for ref in v_refs])
        for i, out in enumerate(outs):
            rows = hidden_ref[:, pl.ds(32 * i, 32), :].reshape(128, 1792)
            out[...] = jnp.dot(rows, v, preferred_element_type=wide).astype(out.dtype)

    return pl.pallas_call(
        kernel,
        grid=(2,),
        in_specs=[pl.BlockSpec((4, 32 * n, 1792), lambda i: (0, 0, 0))]
        + [pl.BlockSpec((448, 512), lambda i: (0, i))] * 4,
        out_specs=[pl.BlockSpec((128, 512), lambda i: (0, i))] * n,
        out_shape=[jax.ShapeDtypeStruct((128, 1024), t) for t in types],
        compiler_params=pltpu.CompilerParams(vmem_limit_bytes=LIMIT),
        cost_estimate=pl.CostEstimate(
            flops=2 * n * 128 * 1792 * 1024, bytes_accessed=1792 * 2048 + n * 128 * 8192, transcendentals=0
        ),
    )(hidden, *weights)


def on_device(tokens, routes, route_gates, w_in, w_down):
    core = lax.axis_index("core")
    zlo = lax.axis_index("zlo")
    expert = zlo * 2 + core

    mine = [tokens[0]] + [shift(tokens[0], "zlo", d) for d in (1, 2, 3)]
    w_own = jnp.transpose(w_in[0], (1, 2, 0)).reshape(896, 1024)
    weights = [w_own] + [shift(w_own, "y", d) for d in (1, 2, 3)]

    matches = routes[:, :, None] == jnp.arange(8, dtype=jnp.int32)[None, None, :]
    hit = jnp.sum(matches.astype(jnp.int32), axis=1)
    slot = jnp.cumsum(hit, axis=0) - hit
    weight = jnp.sum(route_gates[:, :, None] * matches.astype(wide), axis=1)
    names = jnp.arange(8, dtype=jnp.int32)

    def places(e):
        taken = lax.dynamic_index_in_dim(hit, e, 1, keepdims=False)
        place = lax.dynamic_index_in_dim(slot, e, 1, keepdims=False)
        chosen = [(taken == 1) & (place == k) for k in range(2)]
        owner = [jnp.sum(jnp.where(c, names >> 1, 0)) for c in chosen]
        side = [jnp.sum(jnp.where(c, names & 1, 0)) for c in chosen]
        return chosen, owner, side

    chosen, owner, side = places(expert)
    _, owner_too, _ = places(expert + 1 - 2 * core)
    gates = lax.dynamic_index_in_dim(weight, expert, 1, keepdims=False)
    scales = [jnp.sum(jnp.where(c, gates, 0.0)) for c in chosen]

    def taking(owners):
        out = []
        for z in owners:
            away = (zlo - z) & 3
            near = jnp.where(away == 0, mine[0], mine[1])
            out.append(jnp.where(away < 2, near, jnp.where(away == 2, mine[2], mine[3])))
        return out

    other = shift(jnp.concatenate(taking(owner_too)), "core", 1)
    rows = jnp.concatenate(
        [jnp.where(side[k] == core, a, other[64 * k : 64 * k + 64]) for k, a in enumerate(taking(owner))]
    )

    above = shift(rows, "zhi", -1)
    below = shift(rows, "zhi", 1)
    far = onward(jnp.where(core == 0, below, above), "zhi")

    part = gate_up([far, above, below], weights)
    v_own = hold(w_down[0], part)
    v_all = [v_own] + [shift(v_own, "y", d) for d in (1, 2, 3)]
    hidden = swap(activate(swap(part, "x"), v_all[1], v_all[3]), "x")
    far_out, above_out, below_out = down(hidden, v_all, (half, wide, wide))
    got = onward(far_out, "zhi").astype(wide)
    up = shift((above_out + jnp.where(core == 0, got, 0.0)).astype(half), "zhi", 1)
    back = shift((below_out + jnp.where(core == 1, got, 0.0)).astype(half), "zhi", -1)

    own = swap(gate_up([rows], weights, far_out), "x")
    own = swap(activate(own), "x")
    (own_out,) = down(own, v_all, (wide,))
    result = own_out + up.astype(wide) + back.astype(wide)

    def toward(away, parity):
        z = (zlo + away) & 3
        return sum(
            jnp.where((owner[k] == z) & (side[k] == parity), scales[k] * result[64 * k : 64 * k + 64], 0.0)
            for k in range(2)
        )

    got = shift(jnp.concatenate([toward(d, 1 - core).astype(half) for d in range(4)]), "core", 1)
    going = [toward(d, core) + got[64 * d : 64 * d + 64].astype(wide) for d in range(4)]
    total = going[0]
    for d in (1, 2, 3):
        total = total + shift(going[d].astype(half), "zlo", d).astype(wide)
    return total.astype(half)[None]


def solution(mesh):
    fine = Mesh(mesh.devices.reshape(4, 2, 4, 4, 4), ("zlo", "core", "x", "y", "zhi"))
    seqs, pos = ("zlo", "core"), ("y", "zhi")
    return jax.shard_map(
        on_device,
        mesh=fine,
        in_specs=(
            P(seqs, pos, "x"),
            P(),
            P(),
            P(seqs, "x", None, pos),
            P(seqs, pos, "x"),
        ),
        out_specs=P(seqs, pos, "x"),
        check_vma=False,
    )
```

```python
import jax
import jax.numpy as jnp
from jax import lax
from jax.experimental import pallas as pl
from jax.experimental.pallas import tpu as pltpu
from jax.sharding import Mesh, PartitionSpec as P

wide = jnp.float32
half = jnp.bfloat16
LIMIT = 60 * 2**20
COST = pl.CostEstimate(flops=1024, bytes_accessed=1024, transcendentals=0)
ANY = pl.BlockSpec(memory_space=pl.ANY)


def shift(a, axis, by):
    n = lax.axis_size(axis)
    return lax.ppermute(a, axis, [(i, (i + by) % n) for i in range(n)])


def onward(a, axis):
    n = lax.axis_size(axis)
    return lax.ppermute(
        a, ("core", axis), [(c * n + i, c * n + (i + 1 - 2 * c) % n) for c in range(2) for i in range(n)]
    )


def swap(a, axis):
    return lax.all_to_all(a, axis, split_axis=0, concat_axis=0, tiled=True)


def pick(first, second, after):
    rows = first.shape[0] // 7

    def kernel(a_ref, b_ref, core_ref, after_ref, out_ref):
        out_ref[...] = jnp.where(core_ref[0] == 0, a_ref[...], b_ref[...])

    block = pl.BlockSpec((rows, 1024), lambda i: (i, 0))
    return pl.pallas_call(
        kernel,
        grid=(7,),
        in_specs=[block, block, pl.BlockSpec(memory_space=pltpu.SMEM), ANY],
        out_specs=block,
        out_shape=jax.ShapeDtypeStruct(first.shape, first.dtype),
        compiler_params=pltpu.CompilerParams(vmem_limit_bytes=LIMIT),
        cost_estimate=COST,
    )(first, second, lax.axis_index("core").reshape(1), after)


def hold(a, after):
    def kernel(a_ref, after_ref, out_ref):
        out_ref[...] = a_ref[...]

    block = pl.BlockSpec((a.shape[0] // 4, 1024), lambda i: (i, 0))
    return pl.pallas_call(
        kernel,
        grid=(4,),
        in_specs=[block, ANY],
        out_specs=block,
        out_shape=jax.ShapeDtypeStruct(a.shape, a.dtype),
        compiler_params=pltpu.CompilerParams(vmem_limit_bytes=LIMIT),
        cost_estimate=COST,
    )(a, after)


def early(pieces, weights):
    n = len(pieces)

    def kernel(*refs):
        x = jnp.concatenate([ref[...] for ref in refs[:n]])
        w = [ref[...] for ref in refs[n : n + 3]]
        w = jnp.concatenate([a[:448] for a in w] + [a[448:] for a in w])
        out = lax.dot_general(x, w, (((1,), (1,)), ((), ())), preferred_element_type=wide).astype(half)
        for i in range(n):
            refs[-1][:, pl.ds(32 * i, 32), :] = out[128 * i : 128 * i + 128].reshape(4, 32, 2688)

    return pl.pallas_call(
        kernel,
        out_shape=jax.ShapeDtypeStruct((4, 32 * n, 2688), half),
        compiler_params=pltpu.CompilerParams(vmem_limit_bytes=LIMIT),
        cost_estimate=COST,
    )(*pieces, *weights)


def late(far, pieces, weights, after):
    def kernel(far_ref, *refs):
        out_ref = refs[-1]
        w = [ref[...] for ref in refs[3:7]]
        w_all = jnp.concatenate([a[:448] for a in w] + [a[448:] for a in w])
        dims = (((1,), (1,)), ((), ()))
        out = lax.dot_general(far_ref[...], w_all, dims, preferred_element_type=wide).astype(half)
        out_ref[:, :, :3584] = out.reshape(4, 32, 3584)
        x = jnp.concatenate([ref[...] for ref in refs[:3]])
        out = lax.dot_general(x, w[3], dims, preferred_element_type=wide).astype(half)
        for i in range(3):
            out_ref[:, :, pl.ds(3584 + 896 * i, 896)] = out[128 * i : 128 * i + 128].reshape(4, 32, 896)

    whole = pl.BlockSpec(memory_space=pltpu.VMEM)
    return pl.pallas_call(
        kernel,
        in_specs=[whole] * 8 + [ANY] * len(after),
        out_shape=jax.ShapeDtypeStruct((4, 32, 6272), half),
        compiler_params=pltpu.CompilerParams(vmem_limit_bytes=LIMIT),
        cost_estimate=COST,
    )(far, *pieces, *weights, *after)


def act(gate, up):
    return (gate / (1.0 + jnp.exp(-gate)) * up).astype(half)


def activate_early(sums, after):
    rows = sums.shape[1]

    def kernel(sums_ref, after_ref, out_ref):
        total = jnp.sum(sums_ref[...].astype(wide), axis=0)
        out_ref[...] = act(total[:, :1344], total[:, 1344:])

    return pl.pallas_call(
        kernel,
        in_specs=[pl.BlockSpec(memory_space=pltpu.VMEM), ANY],
        out_shape=jax.ShapeDtypeStruct((rows, 1344), half),
        compiler_params=pltpu.CompilerParams(vmem_limit_bytes=LIMIT),
        cost_estimate=COST,
    )(sums, after)


def activate_late(sums, first):
    def kernel(sums_ref, first_ref, *outs):
        total = jnp.sum(sums_ref[...].astype(wide), axis=0)
        parts = [act(total[:, :1792], total[:, 1792:3584])]
        rest = []
        for i in range(3):
            at = 3584 + 896 * i
            rest.append(act(total[:, at : at + 448], total[:, at + 448 : at + 896]))
        whole = jnp.concatenate([first_ref[...], jnp.concatenate(rest)], axis=1)
        parts += [whole[:64], whole[64:]]
        for part, out in zip(parts, outs):
            for j in range(4):
                out[j] = part

    return pl.pallas_call(
        kernel,
        out_shape=[jax.ShapeDtypeStruct((4, r, 1792), half) for r in (32, 64, 32)],
        compiler_params=pltpu.CompilerParams(vmem_limit_bytes=LIMIT),
        cost_estimate=COST,
    )(sums, first)


def down(hidden, weights, types):
    n = len(types)

    def kernel(*refs):
        hidden_ref, v_refs, outs = refs[0], refs[1:5], refs[5:]
        v = jnp.concatenate([ref[...] for ref in v_refs])
        for i, out in enumerate(outs):
            rows = hidden_ref[:, pl.ds(32 * i, 32), :].reshape(128, 1792)
            out[...] = jnp.dot(rows, v, preferred_element_type=wide).astype(out.dtype)

    return pl.pallas_call(
        kernel,
        grid=(2,),
        in_specs=[pl.BlockSpec((4, 32 * n, 1792), lambda i: (0, 0, 0))]
        + [pl.BlockSpec((448, 512), lambda i: (0, i))] * 4,
        out_specs=[pl.BlockSpec((128, 512), lambda i: (0, i))] * n,
        out_shape=[jax.ShapeDtypeStruct((128, 1024), t) for t in types],
        compiler_params=pltpu.CompilerParams(vmem_limit_bytes=LIMIT),
        cost_estimate=COST,
    )(hidden, *weights)


def on_device(tokens, routes, route_gates, w_in, w_down):
    core = lax.axis_index("core")
    zlo = lax.axis_index("zlo")
    expert = zlo * 2 + core

    mine = [tokens[0]] + [shift(tokens[0], "zlo", d) for d in (1, 2, 3)]
    w_own = jnp.transpose(w_in[0], (1, 2, 0)).reshape(896, 1024)
    w_above = shift(w_own, "y", -1)
    w_below = shift(w_own, "y", 1)
    weights = [w_own, w_above, w_below]

    matches = routes[:, :, None] == jnp.arange(8, dtype=jnp.int32)[None, None, :]
    hit = jnp.sum(matches.astype(jnp.int32), axis=1)
    slot = jnp.cumsum(hit, axis=0) - hit
    weight = jnp.sum(route_gates[:, :, None] * matches.astype(wide), axis=1)
    names = jnp.arange(8, dtype=jnp.int32)

    def places(e):
        taken = lax.dynamic_index_in_dim(hit, e, 1, keepdims=False)
        place = lax.dynamic_index_in_dim(slot, e, 1, keepdims=False)
        chosen = [(taken == 1) & (place == k) for k in range(2)]
        owner = [jnp.sum(jnp.where(c, names >> 1, 0)) for c in chosen]
        side = [jnp.sum(jnp.where(c, names & 1, 0)) for c in chosen]
        return chosen, owner, side

    chosen, owner, side = places(expert)
    _, owner_too, _ = places(expert + 1 - 2 * core)
    gates = lax.dynamic_index_in_dim(weight, expert, 1, keepdims=False)
    scales = [jnp.sum(jnp.where(c, gates, 0.0)) for c in chosen]

    def taking(owners):
        out = []
        for z in owners:
            away = (zlo - z) & 3
            near = jnp.where(away == 0, mine[0], mine[1])
            out.append(jnp.where(away < 2, near, jnp.where(away == 2, mine[2], mine[3])))
        return out

    other = shift(jnp.concatenate(taking(owner_too)), "core", 1)
    rows = jnp.concatenate(
        [jnp.where(side[k] == core, a, other[64 * k : 64 * k + 64]) for k, a in enumerate(taking(owner))]
    )

    above = shift(rows, "zhi", -1)
    below = shift(rows, "zhi", 1)
    v_own = hold(w_down[0], rows)
    v_above = shift(v_own, "y", -1)
    v_below = shift(v_own, "y", 1)
    next_z = jnp.where(core == 0, below, above)
    far = onward(next_z, "zhi")
    w_far = onward(pick(w_below, w_above, next_z), "y")
    part = early([above, below, rows], weights)

    v_far = onward(pick(v_below, v_above, part), "y")
    v_all = [v_own, v_above, v_below, v_far]
    first = activate_early(swap(part, "x"), v_far)
    rest = swap(late(far, [above, below, rows], weights + [w_far], [v_above, v_below]), "x")
    far_h, near_h, own_h = activate_late(rest, first)

    (far_out,) = down(swap(far_h, "x"), v_all, (half,))
    got = onward(far_out, "zhi").astype(wide)
    above_out, below_out = down(swap(near_h, "x"), v_all, (wide, wide))
    up = shift((above_out + jnp.where(core == 0, got, 0.0)).astype(half), "zhi", 1)
    back = shift((below_out + jnp.where(core == 1, got, 0.0)).astype(half), "zhi", -1)

    (own_out,) = down(swap(own_h, "x"), v_all, (wide,))
    result = own_out + up.astype(wide) + back.astype(wide)

    def toward(away, parity):
        z = (zlo + away) & 3
        return sum(
            jnp.where((owner[k] == z) & (side[k] == parity), scales[k] * result[64 * k : 64 * k + 64], 0.0)
            for k in range(2)
        )

    got = shift(jnp.concatenate([toward(d, 1 - core).astype(half) for d in range(4)]), "core", 1)
    going = [toward(d, core) + got[64 * d : 64 * d + 64].astype(wide) for d in range(4)]
    total = going[0]
    for d in (1, 2, 3):
        total = total + shift(going[d].astype(half), "zlo", d).astype(wide)
    return total.astype(half)[None]


def solution(mesh):
    fine = Mesh(mesh.devices.reshape(4, 2, 4, 4, 4), ("zlo", "core", "x", "y", "zhi"))
    seqs, pos = ("zlo", "core"), ("y", "zhi")
    return jax.shard_map(
        on_device,
        mesh=fine,
        in_specs=(
            P(seqs, pos, "x"),
            P(),
            P(),
            P(seqs, "x", None, pos),
            P(seqs, pos, "x"),
        ),
        out_specs=P(seqs, pos, "x"),
        check_vma=False,
    )
```

```python
import jax
import jax.numpy as jnp
from jax import lax
from jax.experimental import pallas as pl
from jax.experimental.pallas import tpu as pltpu
from jax.sharding import Mesh, PartitionSpec as P

wide = jnp.float32
half = jnp.bfloat16
LIMIT = 60 * 2**20
COST = pl.CostEstimate(flops=1024, bytes_accessed=1024, transcendentals=0)
ANY = pl.BlockSpec(memory_space=pl.ANY)
WHOLE = pl.BlockSpec(memory_space=pltpu.VMEM)


def shift(a, axis, by):
    n = lax.axis_size(axis)
    return lax.ppermute(a, axis, [(i, (i + by) % n) for i in range(n)])


def pass_on(a, axis, by):
    n = lax.axis_size(axis)
    return lax.ppermute(
        a, ("core", axis), [(c * n + i, c * n + (i + by * (1 - 2 * c)) % n) for c in range(2) for i in range(n)]
    )


def swap(a, axis):
    return lax.all_to_all(a, axis, split_axis=0, concat_axis=0, tiled=True)


DIMS = (((1,), (1,)), ((), ()))


def hold(a, after):
    def kernel(a_ref, after_ref, out_ref):
        out_ref[...] = a_ref[...]

    return pl.pallas_call(
        kernel,
        in_specs=[WHOLE, ANY],
        out_specs=WHOLE,
        out_shape=jax.ShapeDtypeStruct(a.shape, a.dtype),
        compiler_params=pltpu.CompilerParams(vmem_limit_bytes=LIMIT),
        cost_estimate=COST,
    )(a, after)


def fetch(refs, held, sems):
    copies = [pltpu.make_async_copy(ref, held.at[i], sems.at[i]) for i, ref in enumerate(refs)]
    for copy in copies:
        copy.start()
    return copies


def early(pieces, weights, after):
    def kernel(*refs):
        out_ref, copy_ref, held, sems, sem = refs[-5:]
        copies = fetch(refs[3:6], held, sems)
        x = jnp.concatenate([ref[...] for ref in refs[:3]])
        spare = pltpu.make_async_copy(held.at[1], copy_ref, sem)
        for i in range(3):
            copies[i].wait()
            if i == 1:
                spare.start()
            out = lax.dot_general(x, held[i], DIMS, preferred_element_type=wide).astype(half)
            for p in range(3):
                out_ref[:, pl.ds(32 * p, 32), pl.ds(896 * i, 896)] = out[128 * p : 128 * p + 128].reshape(4, 32, 896)
        spare.wait()

    return pl.pallas_call(
        kernel,
        in_specs=[WHOLE] * 3 + [ANY] * (3 + len(after)),
        out_specs=[WHOLE, ANY],
        out_shape=[jax.ShapeDtypeStruct((4, 96, 2688), half), jax.ShapeDtypeStruct((896, 1024), half)],
        scratch_shapes=[
            pltpu.VMEM((3, 896, 1024), half),
            pltpu.SemaphoreType.DMA((3,)),
            pltpu.SemaphoreType.DMA,
        ],
        compiler_params=pltpu.CompilerParams(vmem_limit_bytes=LIMIT),
        cost_estimate=COST,
    )(*pieces, *weights, *after)


def late_near(far, weights):
    def kernel(far_ref, *refs):
        out_ref, held, sums, sems, sem = refs[-5:]
        copies = fetch(refs[:3], held, sems)
        x = far_ref[...]
        for i in range(3):
            copies[i].wait()
            out = lax.dot_general(x, held[i], DIMS, preferred_element_type=wide).astype(half)
            sums[:, :, pl.ds(896 * i, 896)] = out.reshape(4, 32, 896)
        copy = pltpu.make_async_copy(sums, out_ref.at[:, :, pl.ds(0, 2688)], sem)
        copy.start()
        copy.wait()

    return pl.pallas_call(
        kernel,
        in_specs=[WHOLE] + [ANY] * 3,
        out_specs=ANY,
        out_shape=jax.ShapeDtypeStruct((4, 32, 6272), half),
        scratch_shapes=[
            pltpu.VMEM((3, 896, 1024), half),
            pltpu.VMEM((4, 32, 2688), half),
            pltpu.SemaphoreType.DMA((3,)),
            pltpu.SemaphoreType.DMA,
        ],
        compiler_params=pltpu.CompilerParams(vmem_limit_bytes=LIMIT),
        cost_estimate=COST,
    )(far, *weights)


def late_far(pieces, w_far, begun):
    def kernel(*refs):
        w_ref, out_ref, sums, sem = refs[4], refs[6], refs[7], refs[8]
        x = jnp.concatenate([ref[...] for ref in refs[:4]])
        out = lax.dot_general(x, w_ref[...], DIMS, preferred_element_type=wide).astype(half)
        for p in range(4):
            sums[:, :, pl.ds(896 * p, 896)] = out[128 * p : 128 * p + 128].reshape(4, 32, 896)
        copy = pltpu.make_async_copy(sums, out_ref.at[:, :, pl.ds(2688, 3584)], sem)
        copy.start()
        copy.wait()

    return pl.pallas_call(
        kernel,
        in_specs=[WHOLE] * 5 + [ANY],
        out_specs=ANY,
        out_shape=jax.ShapeDtypeStruct((4, 32, 6272), half),
        scratch_shapes=[pltpu.VMEM((4, 32, 3584), half), pltpu.SemaphoreType.DMA],
        input_output_aliases={5: 0},
        compiler_params=pltpu.CompilerParams(vmem_limit_bytes=LIMIT),
        cost_estimate=COST,
    )(*pieces, w_far, begun)


def act(gate, up):
    return (gate / (1.0 + jnp.exp(-gate)) * up).astype(half)


def block(sums, i):
    at = 896 * i
    return act(sums[:, at : at + 448], sums[:, at + 448 : at + 896])


def activate_early(sums, after):
    def kernel(sums_ref, *refs):
        out_ref = refs[-1]
        total = jnp.sum(sums_ref[...].astype(wide), axis=0)
        out_ref[...] = jnp.concatenate([block(total, i) for i in range(3)], axis=1)

    return pl.pallas_call(
        kernel,
        in_specs=[WHOLE] + [ANY] * len(after),
        out_specs=WHOLE,
        out_shape=jax.ShapeDtypeStruct((96, 1344), half),
        compiler_params=pltpu.CompilerParams(vmem_limit_bytes=LIMIT),
        cost_estimate=COST,
    )(sums, *after)


def activate_late(sums, first):
    def kernel(sums_ref, first_ref, *outs):
        total = jnp.sum(sums_ref[...].astype(wide), axis=0)
        blocks = [block(total, i) for i in range(7)]
        far = jnp.concatenate(blocks[:4], axis=1)
        rest = jnp.concatenate([first_ref[...], jnp.concatenate(blocks[4:])], axis=1)
        for part, out in zip((far, rest[:64], rest[64:]), outs):
            for j in range(4):
                out[j] = part

    return pl.pallas_call(
        kernel,
        out_shape=[jax.ShapeDtypeStruct((4, r, 1792), half) for r in (32, 64, 32)],
        compiler_params=pltpu.CompilerParams(vmem_limit_bytes=LIMIT),
        cost_estimate=COST,
    )(sums, first)


def down(hidden, weights, types):
    n = len(types)

    def kernel(*refs):
        hidden_ref, v_refs, outs = refs[0], refs[1:5], refs[5:]
        v = jnp.concatenate([ref[...] for ref in v_refs])
        for i, out in enumerate(outs):
            rows = hidden_ref[:, pl.ds(32 * i, 32), :].reshape(128, 1792)
            out[...] = jnp.dot(rows, v, preferred_element_type=wide).astype(out.dtype)

    return pl.pallas_call(
        kernel,
        grid=(2,),
        in_specs=[pl.BlockSpec((4, 32 * n, 1792), lambda i: (0, 0, 0))]
        + [pl.BlockSpec((448, 512), lambda i: (0, i))] * 4,
        out_specs=[pl.BlockSpec((128, 512), lambda i: (0, i))] * n,
        out_shape=[jax.ShapeDtypeStruct((128, 1024), t) for t in types],
        compiler_params=pltpu.CompilerParams(vmem_limit_bytes=LIMIT),
        cost_estimate=COST,
    )(hidden, *weights)


def on_device(tokens, routes, route_gates, w_in, w_down):
    core = lax.axis_index("core")
    zlo = lax.axis_index("zlo")
    expert = zlo * 2 + core

    mine = [tokens[0]] + [shift(tokens[0], "zlo", d) for d in (1, 2, 3)]
    w_own, v_own = jnp.transpose(w_in[0], (1, 2, 0)).reshape(896, 1024), w_down[0]
    w_first, w_second = pass_on(w_own, "y", 1), pass_on(w_own, "y", -1)
    v_first, v_second = pass_on(v_own, "y", 1), pass_on(v_own, "y", -1)
    weights = [w_own, w_first, w_second]

    matches = routes[:, :, None] == jnp.arange(8, dtype=jnp.int32)[None, None, :]
    hit = jnp.sum(matches.astype(jnp.int32), axis=1)
    slot = jnp.cumsum(hit, axis=0) - hit
    weight = jnp.sum(route_gates[:, :, None] * matches.astype(wide), axis=1)
    names = jnp.arange(8, dtype=jnp.int32)

    def places(e):
        taken = lax.dynamic_index_in_dim(hit, e, 1, keepdims=False)
        place = lax.dynamic_index_in_dim(slot, e, 1, keepdims=False)
        chosen = [(taken == 1) & (place == k) for k in range(2)]
        owner = [jnp.sum(jnp.where(c, names >> 1, 0)) for c in chosen]
        side = [jnp.sum(jnp.where(c, names & 1, 0)) for c in chosen]
        return chosen, owner, side

    chosen, owner, side = places(expert)
    _, owner_too, _ = places(expert + 1 - 2 * core)
    gates = lax.dynamic_index_in_dim(weight, expert, 1, keepdims=False)
    scales = [jnp.sum(jnp.where(c, gates, 0.0)) for c in chosen]

    def taking(owners):
        out = []
        for z in owners:
            away = (zlo - z) & 3
            near = jnp.where(away == 0, mine[0], mine[1])
            out.append(jnp.where(away < 2, near, jnp.where(away == 2, mine[2], mine[3])))
        return out

    other = shift(jnp.concatenate(taking(owner_too)), "core", 1)
    rows = jnp.concatenate(
        [jnp.where(side[k] == core, a, other[64 * k : 64 * k + 64]) for k, a in enumerate(taking(owner))]
    )

    first, second = pass_on(rows, "zhi", 1), pass_on(rows, "zhi", -1)
    part, w_next = early([first, second, rows], weights, [v_first])

    far = pass_on(hold(first, second), "zhi", 1)
    w_far = pass_on(w_next, "y", 1)
    v_far = pass_on(v_first, "y", 1)
    v_all = [v_own, v_first, v_second, v_far]
    begun = activate_early(swap(part, "x"), [v_second, v_far])
    rest = swap(late_far([far, first, second, rows], w_far, late_near(far, weights)), "x")
    far_h, near_h, own_h = activate_late(rest, begun)

    (far_out,) = down(swap(far_h, "x"), v_all, (half,))
    got = pass_on(far_out, "zhi", 1)
    first_out, second_out = down(swap(near_h, "x"), v_all, (half, wide))
    back = pass_on(first_out, "zhi", -1)
    ahead = pass_on((second_out + got.astype(wide)).astype(half), "zhi", 1)

    (own_out,) = down(swap(own_h, "x"), v_all, (wide,))
    result = (own_out + ahead.astype(wide) + back.astype(wide)).reshape(2, 64, 1024)

    ids = jnp.arange(4, dtype=jnp.int32)[:, None, None]

    def toward(parity):
        return sum(
            jnp.where((owner[k] == ids) & (side[k] == parity), scales[k] * result[k][None], 0.0)
            for k in range(2)
        )

    got = shift(toward(1 - core).astype(half), "core", 1)
    going = (toward(core) + got.astype(wide)).astype(half)
    return jnp.sum(swap(going, "zlo").astype(wide), axis=0, keepdims=True).astype(half)


def solution(mesh):
    fine = Mesh(mesh.devices.reshape(4, 2, 4, 4, 4), ("zlo", "core", "x", "y", "zhi"))
    seqs, pos = ("zlo", "core"), ("y", "zhi")
    return jax.shard_map(
        on_device,
        mesh=fine,
        in_specs=(
            P(seqs, pos, "x"),
            P(),
            P(),
            P(seqs, "x", None, pos),
            P(seqs, pos, "x"),
        ),
        out_specs=P(seqs, pos, "x"),
        check_vma=False,
    )
```

```python
import jax
import jax.numpy as jnp
from jax import lax
from jax.experimental import pallas as pl
from jax.experimental.pallas import tpu as pltpu
from jax.sharding import Mesh, PartitionSpec as P

wide = jnp.float32
half = jnp.bfloat16
LIMIT = 60 * 2**20
COST = pl.CostEstimate(flops=1024, bytes_accessed=1024, transcendentals=0)
ANY = pl.BlockSpec(memory_space=pl.ANY)
WHOLE = pl.BlockSpec(memory_space=pltpu.VMEM)


def shift(a, axis, by):
    n = lax.axis_size(axis)
    return lax.ppermute(a, axis, [(i, (i + by) % n) for i in range(n)])


def pass_on(a, axis, by):
    n = lax.axis_size(axis)
    return lax.ppermute(
        a, ("core", axis), [(c * n + i, c * n + (i + by * (1 - 2 * c)) % n) for c in range(2) for i in range(n)]
    )


def swap(a, axis):
    return lax.all_to_all(a, axis, split_axis=0, concat_axis=0, tiled=True)


DIMS = (((1,), (1,)), ((), ()))


def fetch(refs, held, sems):
    copies = [pltpu.make_async_copy(ref, held.at[i], sems.at[i]) for i, ref in enumerate(refs)]
    for copy in copies:
        copy.start()
    return copies


def early(pieces, weights):
    def kernel(*refs):
        out_ref, piece_ref, copy_ref, held, sums, sems, out_sems, sem, piece_sem = refs[-9:]
        copies = fetch(refs[3:6], held, sems)
        piece = pltpu.make_async_copy(refs[0], piece_ref, piece_sem)
        piece.start()
        x = jnp.concatenate([ref[...] for ref in refs[:3]])
        spare = pltpu.make_async_copy(held.at[1], copy_ref, sem)
        going = []
        for i in range(3):
            copies[i].wait()
            if i == 1:
                spare.start()
            columns = pl.ds(896 * i, 896)
            out = lax.dot_general(x, held[i], DIMS, preferred_element_type=wide).astype(half)
            for p in range(3):
                sums[:, pl.ds(32 * p, 32), columns] = out[128 * p : 128 * p + 128].reshape(4, 32, 896)
            going.append(pltpu.make_async_copy(sums.at[:, :, columns], out_ref.at[:, :, columns], out_sems.at[i]))
            going[i].start()
        for copy in going + [spare, piece]:
            copy.wait()

    return pl.pallas_call(
        kernel,
        in_specs=[WHOLE] * 3 + [ANY] * 3,
        out_specs=[ANY] * 3,
        out_shape=[
            jax.ShapeDtypeStruct((4, 96, 2688), half),
            jax.ShapeDtypeStruct((128, 1024), half),
            jax.ShapeDtypeStruct((896, 1024), half),
        ],
        scratch_shapes=[
            pltpu.VMEM((3, 896, 1024), half),
            pltpu.VMEM((4, 96, 2688), half),
            pltpu.SemaphoreType.DMA((3,)),
            pltpu.SemaphoreType.DMA((3,)),
            pltpu.SemaphoreType.DMA,
            pltpu.SemaphoreType.DMA,
        ],
        compiler_params=pltpu.CompilerParams(vmem_limit_bytes=LIMIT),
        cost_estimate=COST,
    )(*pieces, *weights)


def late_near(far, weights):
    def kernel(far_ref, *refs):
        out_ref, held, sums, sems, sem = refs[-5:]
        copies = fetch(refs[:3], held, sems)
        x = far_ref[...]
        for i in range(3):
            copies[i].wait()
            out = lax.dot_general(x, held[i], DIMS, preferred_element_type=wide).astype(half)
            sums[:, :, pl.ds(896 * i, 896)] = out.reshape(4, 32, 896)
        copy = pltpu.make_async_copy(sums, out_ref.at[:, :, pl.ds(0, 2688)], sem)
        copy.start()
        copy.wait()

    return pl.pallas_call(
        kernel,
        in_specs=[WHOLE] + [ANY] * 3,
        out_specs=ANY,
        out_shape=jax.ShapeDtypeStruct((4, 32, 6272), half),
        scratch_shapes=[
            pltpu.VMEM((3, 896, 1024), half),
            pltpu.VMEM((4, 32, 2688), half),
            pltpu.SemaphoreType.DMA((3,)),
            pltpu.SemaphoreType.DMA,
        ],
        compiler_params=pltpu.CompilerParams(vmem_limit_bytes=LIMIT),
        cost_estimate=COST,
    )(far, *weights)


def late_far(pieces, w_far, begun):
    def kernel(*refs):
        w_ref, out_ref, sums, sem = refs[4], refs[6], refs[7], refs[8]
        x = jnp.concatenate([ref[...] for ref in refs[:4]])
        out = lax.dot_general(x, w_ref[...], DIMS, preferred_element_type=wide).astype(half)
        for p in range(4):
            sums[:, :, pl.ds(896 * p, 896)] = out[128 * p : 128 * p + 128].reshape(4, 32, 896)
        copy = pltpu.make_async_copy(sums, out_ref.at[:, :, pl.ds(2688, 3584)], sem)
        copy.start()
        copy.wait()

    return pl.pallas_call(
        kernel,
        in_specs=[WHOLE] * 5 + [ANY],
        out_specs=ANY,
        out_shape=jax.ShapeDtypeStruct((4, 32, 6272), half),
        scratch_shapes=[pltpu.VMEM((4, 32, 3584), half), pltpu.SemaphoreType.DMA],
        input_output_aliases={5: 0},
        compiler_params=pltpu.CompilerParams(vmem_limit_bytes=LIMIT),
        cost_estimate=COST,
    )(*pieces, w_far, begun)


def act(gate, up):
    return (gate / (1.0 + jnp.exp(-gate)) * up).astype(half)


def block(sums, i):
    at = 896 * i
    return act(sums[:, at : at + 448], sums[:, at + 448 : at + 896])


def activate_early(sums):
    def kernel(sums_ref, out_ref):
        total = jnp.sum(sums_ref[...].astype(wide), axis=0)
        out_ref[...] = jnp.concatenate([block(total, i) for i in range(3)], axis=1)

    return pl.pallas_call(
        kernel,
        grid=(1,),
        in_specs=[pl.BlockSpec((4, 96, 2688), lambda i: (0, 0, 0))],
        out_specs=pl.BlockSpec((96, 1344), lambda i: (0, 0)),
        out_shape=jax.ShapeDtypeStruct((96, 1344), half),
        compiler_params=pltpu.CompilerParams(vmem_limit_bytes=LIMIT),
        cost_estimate=COST,
    )(sums)


def activate_late(sums, begun, after):
    def kernel(sums_ref, begun_ref, *refs):
        others_ref, own_ref = refs[-2:]
        total = jnp.sum(sums_ref[...].astype(wide), axis=0)
        blocks = [block(total, i) for i in range(7)]
        far = jnp.concatenate(blocks[:4], axis=1)
        rest = jnp.concatenate([begun_ref[...], jnp.concatenate(blocks[4:])], axis=1)
        for j in range(4):
            others_ref[j, :32] = far
            others_ref[j, 32:] = rest[:64]
            own_ref[j] = rest[64:]

    return pl.pallas_call(
        kernel,
        grid=(1,),
        in_specs=[
            pl.BlockSpec((4, 32, 6272), lambda i: (0, 0, 0)),
            pl.BlockSpec((96, 1344), lambda i: (0, 0)),
        ]
        + [ANY] * len(after),
        out_specs=[pl.BlockSpec((4, r, 1792), lambda i: (0, 0, 0)) for r in (96, 32)],
        out_shape=[jax.ShapeDtypeStruct((4, r, 1792), half) for r in (96, 32)],
        compiler_params=pltpu.CompilerParams(vmem_limit_bytes=LIMIT),
        cost_estimate=COST,
    )(sums, begun, *after)


def down(hidden, weights, types):
    n = len(types)

    def kernel(*refs):
        hidden_ref, v_refs, outs = refs[0], refs[1:5], refs[5:]
        v = jnp.concatenate([ref[...] for ref in v_refs])
        for i, out in enumerate(outs):
            rows = hidden_ref[:, pl.ds(32 * i, 32), :].reshape(128, 1792)
            out[...] = jnp.dot(rows, v, preferred_element_type=wide).astype(out.dtype)

    return pl.pallas_call(
        kernel,
        grid=(2,),
        in_specs=[pl.BlockSpec((4, 32 * n, 1792), lambda i: (0, 0, 0))]
        + [pl.BlockSpec((448, 512), lambda i: (0, i))] * 4,
        out_specs=[pl.BlockSpec((128, 512), lambda i: (0, i))] * n,
        out_shape=[jax.ShapeDtypeStruct((128, 1024), t) for t in types],
        compiler_params=pltpu.CompilerParams(vmem_limit_bytes=LIMIT),
        cost_estimate=COST,
    )(hidden, *weights)


def on_device(tokens, routes, route_gates, w_in, w_down):
    core = lax.axis_index("core")
    zlo = lax.axis_index("zlo")
    expert = zlo * 2 + core

    mine = [tokens[0]] + [shift(tokens[0], "zlo", d) for d in (1, 2, 3)]
    w_own, v_own = jnp.transpose(w_in[0], (1, 2, 0)).reshape(896, 1024), w_down[0]
    w_first, w_second = pass_on(w_own, "y", 1), pass_on(w_own, "y", -1)
    v_first, v_second = pass_on(v_own, "y", 1), pass_on(v_own, "y", -1)
    weights = [w_own, w_first, w_second]

    matches = routes[:, :, None] == jnp.arange(8, dtype=jnp.int32)[None, None, :]
    hit = jnp.sum(matches.astype(jnp.int32), axis=1)
    slot = jnp.cumsum(hit, axis=0) - hit
    weight = jnp.sum(route_gates[:, :, None] * matches.astype(wide), axis=1)
    names = jnp.arange(8, dtype=jnp.int32)

    def places(e):
        taken = lax.dynamic_index_in_dim(hit, e, 1, keepdims=False)
        place = lax.dynamic_index_in_dim(slot, e, 1, keepdims=False)
        chosen = [(taken == 1) & (place == k) for k in range(2)]
        owner = [jnp.sum(jnp.where(c, names >> 1, 0)) for c in chosen]
        side = [jnp.sum(jnp.where(c, names & 1, 0)) for c in chosen]
        return chosen, owner, side

    chosen, owner, side = places(expert)
    _, owner_too, _ = places(expert + 1 - 2 * core)
    gates = lax.dynamic_index_in_dim(weight, expert, 1, keepdims=False)
    scales = [jnp.sum(jnp.where(c, gates, 0.0)) for c in chosen]

    def taking(owners):
        out = []
        for z in owners:
            away = (zlo - z) & 3
            near = jnp.where(away == 0, mine[0], mine[1])
            out.append(jnp.where(away < 2, near, jnp.where(away == 2, mine[2], mine[3])))
        return out

    other = shift(jnp.concatenate(taking(owner_too)), "core", 1)
    rows = jnp.concatenate(
        [jnp.where(side[k] == core, a, other[64 * k : 64 * k + 64]) for k, a in enumerate(taking(owner))]
    )

    first, second = pass_on(rows, "zhi", 1), pass_on(rows, "zhi", -1)
    part, z_next, w_next = early([first, second, rows], weights)

    far, w_far, v_far = pass_on(z_next, "zhi", 1), pass_on(w_next, "y", 1), pass_on(v_first, "y", 1)
    v_all = [v_own, v_first, v_second, v_far]
    begun = activate_early(swap(part, "x"))
    rest = swap(late_far([far, first, second, rows], w_far, late_near(far, weights)), "x")
    others_h, own_h = activate_late(rest, begun, [v_first, v_second])

    far_out, first_out, second_out = down(swap(others_h, "x"), v_all, (half, half, wide))
    got = pass_on(far_out, "zhi", 1)
    back = pass_on(first_out, "zhi", -1)
    ahead = pass_on((second_out + got.astype(wide)).astype(half), "zhi", 1)

    (own_out,) = down(swap(own_h, "x"), v_all, (wide,))
    result = (own_out + ahead.astype(wide) + back.astype(wide)).reshape(2, 64, 1024)

    ids = jnp.arange(4, dtype=jnp.int32)[:, None, None]

    def toward(parity):
        return sum(
            jnp.where((owner[k] == ids) & (side[k] == parity), scales[k] * result[k][None], 0.0)
            for k in range(2)
        )

    got = shift(toward(1 - core).astype(half), "core", 1)
    going = (toward(core) + got.astype(wide)).astype(half)
    return jnp.sum(swap(going, "zlo").astype(wide), axis=0, keepdims=True).astype(half)


def solution(mesh):
    fine = Mesh(mesh.devices.reshape(4, 2, 4, 4, 4), ("zlo", "core", "x", "y", "zhi"))
    seqs, pos = ("zlo", "core"), ("y", "zhi")
    return jax.shard_map(
        on_device,
        mesh=fine,
        in_specs=(
            P(seqs, pos, "x"),
            P(),
            P(),
            P(seqs, "x", None, pos),
            P(seqs, pos, "x"),
        ),
        out_specs=P(seqs, pos, "x"),
        check_vma=False,
    )
```

```python
import jax
import jax.numpy as jnp
from jax import lax
from jax.experimental import pallas as pl
from jax.experimental.pallas import tpu as pltpu
from jax.sharding import Mesh, PartitionSpec as P

wide = jnp.float32
half = jnp.bfloat16
LIMIT = 60 * 2**20
COST = pl.CostEstimate(flops=1024, bytes_accessed=1024, transcendentals=0)
ANY = pl.BlockSpec(memory_space=pl.ANY)
WHOLE = pl.BlockSpec(memory_space=pltpu.VMEM)


def shift(a, axis, by):
    n = lax.axis_size(axis)
    return lax.ppermute(a, axis, [(i, (i + by) % n) for i in range(n)])


def pass_on(a, axis, by):
    n = lax.axis_size(axis)
    return lax.ppermute(
        a, ("core", axis), [(c * n + i, c * n + (i + by * (1 - 2 * c)) % n) for c in range(2) for i in range(n)]
    )


def swap(a, axis):
    return lax.all_to_all(a, axis, split_axis=0, concat_axis=0, tiled=True)


DIMS = (((1,), (1,)), ((), ()))


def fetch(refs, held, sems):
    copies = [pltpu.make_async_copy(ref, held.at[i], sems.at[i]) for i, ref in enumerate(refs)]
    for copy in copies:
        copy.start()
    return copies


def early(pieces, weights, after):
    def kernel(*refs):
        out_ref, piece_ref, copy_ref, held, sums, sems, out_sems, sem, piece_sem = refs[-9:]
        copies = fetch(refs[3:6], held, sems)
        piece = pltpu.make_async_copy(refs[0], piece_ref, piece_sem)
        piece.start()
        x = jnp.concatenate([ref[...] for ref in refs[:3]])
        spare = pltpu.make_async_copy(held.at[1], copy_ref, sem)
        going = []
        for i in range(3):
            copies[i].wait()
            if i == 1:
                spare.start()
            columns = pl.ds(896 * i, 896)
            out = lax.dot_general(x, held[i], DIMS, preferred_element_type=wide).astype(half)
            for p in range(3):
                sums[:, pl.ds(32 * p, 32), columns] = out[128 * p : 128 * p + 128].reshape(4, 32, 896)
            going.append(pltpu.make_async_copy(sums.at[:, :, columns], out_ref.at[:, :, columns], out_sems.at[i]))
            going[i].start()
        for copy in going + [spare, piece]:
            copy.wait()

    return pl.pallas_call(
        kernel,
        in_specs=[WHOLE] * 3 + [ANY] * 4,
        out_specs=[ANY] * 3,
        out_shape=[
            jax.ShapeDtypeStruct((4, 96, 2688), half),
            jax.ShapeDtypeStruct((128, 1024), half),
            jax.ShapeDtypeStruct((896, 1024), half),
        ],
        scratch_shapes=[
            pltpu.VMEM((3, 896, 1024), half),
            pltpu.VMEM((4, 96, 2688), half),
            pltpu.SemaphoreType.DMA((3,)),
            pltpu.SemaphoreType.DMA((3,)),
            pltpu.SemaphoreType.DMA,
            pltpu.SemaphoreType.DMA,
        ],
        compiler_params=pltpu.CompilerParams(vmem_limit_bytes=LIMIT),
        cost_estimate=COST,
    )(*pieces, *weights, after)


def late_near(far, weights):
    def kernel(far_ref, *refs):
        out_ref, held, sums, sems, sem = refs[-5:]
        copies = fetch(refs[:3], held, sems)
        x = far_ref[...]
        for i in range(3):
            copies[i].wait()
            out = lax.dot_general(x, held[i], DIMS, preferred_element_type=wide).astype(half)
            sums[:, :, pl.ds(896 * i, 896)] = out.reshape(4, 32, 896)
        copy = pltpu.make_async_copy(sums, out_ref.at[:, :, pl.ds(0, 2688)], sem)
        copy.start()
        copy.wait()

    return pl.pallas_call(
        kernel,
        in_specs=[WHOLE] + [ANY] * 3,
        out_specs=ANY,
        out_shape=jax.ShapeDtypeStruct((4, 32, 6272), half),
        scratch_shapes=[
            pltpu.VMEM((3, 896, 1024), half),
            pltpu.VMEM((4, 32, 2688), half),
            pltpu.SemaphoreType.DMA((3,)),
            pltpu.SemaphoreType.DMA,
        ],
        compiler_params=pltpu.CompilerParams(vmem_limit_bytes=LIMIT),
        cost_estimate=COST,
    )(far, *weights)


def late_far(pieces, w_far, begun):
    def kernel(*refs):
        w_ref, out_ref, sums, sem = refs[4], refs[6], refs[7], refs[8]
        x = jnp.concatenate([ref[...] for ref in refs[:4]])
        out = lax.dot_general(x, w_ref[...], DIMS, preferred_element_type=wide).astype(half)
        for p in range(4):
            sums[:, :, pl.ds(896 * p, 896)] = out[128 * p : 128 * p + 128].reshape(4, 32, 896)
        copy = pltpu.make_async_copy(sums, out_ref.at[:, :, pl.ds(2688, 3584)], sem)
        copy.start()
        copy.wait()

    return pl.pallas_call(
        kernel,
        in_specs=[WHOLE] * 5 + [ANY],
        out_specs=ANY,
        out_shape=jax.ShapeDtypeStruct((4, 32, 6272), half),
        scratch_shapes=[pltpu.VMEM((4, 32, 3584), half), pltpu.SemaphoreType.DMA],
        input_output_aliases={5: 0},
        compiler_params=pltpu.CompilerParams(vmem_limit_bytes=LIMIT),
        cost_estimate=COST,
    )(*pieces, w_far, begun)


def act(gate, up):
    return (gate / (1.0 + jnp.exp(-gate)) * up).astype(half)


def block(sums, i):
    at = 896 * i
    return act(sums[:, at : at + 448], sums[:, at + 448 : at + 896])


def activate_early(sums):
    def kernel(sums_ref, out_ref):
        total = jnp.sum(sums_ref[...].astype(wide), axis=0)
        out_ref[...] = jnp.concatenate([block(total, i) for i in range(3)], axis=1)

    return pl.pallas_call(
        kernel,
        grid=(1,),
        in_specs=[pl.BlockSpec((4, 96, 2688), lambda i: (0, 0, 0))],
        out_specs=pl.BlockSpec((96, 1344), lambda i: (0, 0)),
        out_shape=jax.ShapeDtypeStruct((96, 1344), half),
        compiler_params=pltpu.CompilerParams(vmem_limit_bytes=LIMIT),
        cost_estimate=COST,
    )(sums)


def activate_late(sums, begun, after):
    def kernel(sums_ref, begun_ref, *refs):
        far_ref, near_ref, own_ref = refs[-3:]
        total = jnp.sum(sums_ref[...].astype(wide), axis=0)
        blocks = [block(total, i) for i in range(7)]
        far = jnp.concatenate(blocks[:4], axis=1)
        rest = jnp.concatenate([begun_ref[...], jnp.concatenate(blocks[4:])], axis=1)
        for j in range(4):
            far_ref[j] = far
            near_ref[j] = rest[:64]
            own_ref[j] = rest[64:]

    return pl.pallas_call(
        kernel,
        grid=(1,),
        in_specs=[
            pl.BlockSpec((4, 32, 6272), lambda i: (0, 0, 0)),
            pl.BlockSpec((96, 1344), lambda i: (0, 0)),
        ]
        + [ANY] * len(after),
        out_specs=[pl.BlockSpec((4, r, 1792), lambda i: (0, 0, 0)) for r in (32, 64, 32)],
        out_shape=[jax.ShapeDtypeStruct((4, r, 1792), half) for r in (32, 64, 32)],
        compiler_params=pltpu.CompilerParams(vmem_limit_bytes=LIMIT),
        cost_estimate=COST,
    )(sums, begun, *after)


def down(hidden, weights, types):
    n = len(types)

    def kernel(*refs):
        hidden_ref, v_refs, outs = refs[0], refs[1:5], refs[5:]
        v = jnp.concatenate([ref[...] for ref in v_refs])
        for i, out in enumerate(outs):
            rows = hidden_ref[:, pl.ds(32 * i, 32), :].reshape(128, 1792)
            out[...] = jnp.dot(rows, v, preferred_element_type=wide).astype(out.dtype)

    return pl.pallas_call(
        kernel,
        grid=(2,),
        in_specs=[pl.BlockSpec((4, 32 * n, 1792), lambda i: (0, 0, 0))]
        + [pl.BlockSpec((448, 512), lambda i: (0, i))] * 4,
        out_specs=[pl.BlockSpec((128, 512), lambda i: (0, i))] * n,
        out_shape=[jax.ShapeDtypeStruct((128, 1024), t) for t in types],
        compiler_params=pltpu.CompilerParams(vmem_limit_bytes=LIMIT),
        cost_estimate=COST,
    )(hidden, *weights)


def on_device(tokens, routes, route_gates, w_in, w_down):
    core = lax.axis_index("core")
    zlo = lax.axis_index("zlo")
    expert = zlo * 2 + core

    mine = swap(jnp.broadcast_to(tokens, (4, 64, 1024)), "zlo")
    w_own, v_own = jnp.transpose(w_in[0], (1, 2, 0)).reshape(896, 1024), w_down[0]
    w_first, w_second = pass_on(w_own, "y", 1), pass_on(w_own, "y", -1)
    v_first, v_second = pass_on(v_own, "y", 1), pass_on(v_own, "y", -1)
    weights = [w_own, w_first, w_second]

    matches = routes[:, :, None] == jnp.arange(8, dtype=jnp.int32)[None, None, :]
    hit = jnp.sum(matches.astype(jnp.int32), axis=1)
    slot = jnp.cumsum(hit, axis=0) - hit
    weight = jnp.sum(route_gates[:, :, None] * matches.astype(wide), axis=1)
    names = jnp.arange(8, dtype=jnp.int32)

    def places(e):
        taken = lax.dynamic_index_in_dim(hit, e, 1, keepdims=False)
        place = lax.dynamic_index_in_dim(slot, e, 1, keepdims=False)
        chosen = [(taken == 1) & (place == k) for k in range(2)]
        owner = [jnp.sum(jnp.where(c, names >> 1, 0)) for c in chosen]
        side = [jnp.sum(jnp.where(c, names & 1, 0)) for c in chosen]
        return chosen, owner, side

    chosen, owner, side = places(expert)
    _, owner_too, _ = places(expert + 1 - 2 * core)
    gates = lax.dynamic_index_in_dim(weight, expert, 1, keepdims=False)
    scales = [jnp.sum(jnp.where(c, gates, 0.0)) for c in chosen]

    def taking(owners):
        return [lax.dynamic_index_in_dim(mine, z, 0, keepdims=False) for z in owners]

    other = shift(jnp.concatenate(taking(owner_too)), "core", 1)
    rows = jnp.concatenate(
        [jnp.where(side[k] == core, a, other[64 * k : 64 * k + 64]) for k, a in enumerate(taking(owner))]
    )

    first, second = pass_on(rows, "zhi", 1), pass_on(rows, "zhi", -1)
    part, z_next, w_next = early([first, second, rows], weights, v_first)

    far, w_far, v_far = pass_on(z_next, "zhi", 1), pass_on(w_next, "y", 1), pass_on(v_first, "y", 1)
    v_all = [v_own, v_first, v_second, v_far]
    begun = activate_early(swap(part, "x"))
    rest = swap(late_far([far, first, second, rows], w_far, late_near(far, weights)), "x")
    far_h, near_h, own_h = activate_late(rest, begun, [v_second, v_far])

    (far_out,) = down(swap(far_h, "x"), v_all, (half,))
    got = pass_on(far_out, "zhi", 1)
    first_out, second_out = down(swap(near_h, "x"), v_all, (half, wide))
    back = pass_on(first_out, "zhi", -1)
    ahead = pass_on((second_out + got.astype(wide)).astype(half), "zhi", 1)

    (own_out,) = down(swap(own_h, "x"), v_all, (wide,))
    result = (own_out + ahead.astype(wide) + back.astype(wide)).reshape(2, 64, 1024)

    ids = jnp.arange(4, dtype=jnp.int32)[:, None, None]

    def toward(parity):
        return sum(
            jnp.where((owner[k] == ids) & (side[k] == parity), scales[k] * result[k][None], 0.0)
            for k in range(2)
        )

    got = shift(toward(1 - core).astype(half), "core", 1)
    going = (toward(core) + got.astype(wide)).astype(half)
    return jnp.sum(swap(going, "zlo").astype(wide), axis=0, keepdims=True).astype(half)


def solution(mesh):
    fine = Mesh(mesh.devices.reshape(4, 2, 4, 4, 4), ("zlo", "core", "x", "y", "zhi"))
    seqs, pos = ("zlo", "core"), ("y", "zhi")
    return jax.shard_map(
        on_device,
        mesh=fine,
        in_specs=(
            P(seqs, pos, "x"),
            P(),
            P(),
            P(seqs, "x", None, pos),
            P(seqs, pos, "x"),
        ),
        out_specs=P(seqs, pos, "x"),
        check_vma=False,
    )
```

```python
import jax
import jax.numpy as jnp
from jax import lax
from jax.experimental import pallas as pl
from jax.experimental.pallas import tpu as pltpu
from jax.sharding import Mesh, PartitionSpec as P

wide = jnp.float32
half = jnp.bfloat16
LIMIT = 60 * 2**20
LONG = pl.CostEstimate(flops=10**11, bytes_accessed=1024, transcendentals=0)
COST = pl.CostEstimate(flops=1024, bytes_accessed=1024, transcendentals=0)
ANY = pl.BlockSpec(memory_space=pl.ANY)
WHOLE = pl.BlockSpec(memory_space=pltpu.VMEM)


def shift(a, axis, by):
    n = lax.axis_size(axis)
    return lax.ppermute(a, axis, [(i, (i + by) % n) for i in range(n)])


def pass_on(a, axis, by):
    n = lax.axis_size(axis)
    return lax.ppermute(
        a, ("core", axis), [(c * n + i, c * n + (i + by * (1 - 2 * c)) % n) for c in range(2) for i in range(n)]
    )


def swap(a, axis):
    return lax.all_to_all(a, axis, split_axis=0, concat_axis=0, tiled=True)


DIMS = (((1,), (1,)), ((), ()))


def fetch(refs, held, sems):
    copies = [pltpu.make_async_copy(ref, held.at[i], sems.at[i]) for i, ref in enumerate(refs)]
    for copy in copies:
        copy.start()
    return copies


def early(pieces, weights, spare, after):
    n = len(pieces)

    def kernel(*refs):
        out_ref, held, sums, sems, out_sems = refs[-5:]
        copies = fetch(refs[n : n + 3], held, sems)
        x = jnp.concatenate([ref[...] for ref in refs[:n]])
        going = []
        for i in range(3):
            copies[i].wait()
            if i == 1 and spare:
                going.append(pltpu.make_async_copy(held.at[1], refs[-6], out_sems.at[3]))
                going[-1].start()
            columns = pl.ds(896 * i, 896)
            out = lax.dot_general(x, held[i], DIMS, preferred_element_type=wide).astype(half)
            for p in range(n):
                sums[:, pl.ds(32 * p, 32), columns] = out[128 * p : 128 * p + 128].reshape(4, 32, 896)
            going.append(pltpu.make_async_copy(sums.at[:, :, columns], out_ref.at[:, :, columns], out_sems.at[i]))
            going[-1].start()
        for copy in going:
            copy.wait()

    shapes = [(896, 1024)] * spare + [(4, 32 * n, 2688)]
    return pl.pallas_call(
        kernel,
        in_specs=[WHOLE] * n + [ANY] * (3 + len(after)),
        out_specs=[ANY] * len(shapes),
        out_shape=[jax.ShapeDtypeStruct(shape, half) for shape in shapes],
        scratch_shapes=[
            pltpu.VMEM((3, 896, 1024), half),
            pltpu.VMEM((4, 32 * n, 2688), half),
            pltpu.SemaphoreType.DMA((3,)),
            pltpu.SemaphoreType.DMA((4,)),
        ],
        compiler_params=pltpu.CompilerParams(vmem_limit_bytes=LIMIT),
        cost_estimate=LONG,
    )(*pieces, *weights, *after)


def late(pieces, weights, after):
    def kernel(*refs):
        out_ref, held, sums, sems, out_sems = refs[-5:]
        copies = fetch(refs[4:8], held, sems)
        x = jnp.concatenate([ref[...] for ref in refs[:4]])
        going = []
        for i in range(4):
            copies[i].wait()
            rows = x[:128] if i < 3 else x
            out = lax.dot_general(rows, held[i], DIMS, preferred_element_type=wide).astype(half)
            for p in range(1 if i < 3 else 4):
                columns = pl.ds(896 * (i + p), 896)
                sums[:, :, columns] = out[128 * p : 128 * p + 128].reshape(4, 32, 896)
            columns = pl.ds(896 * i, 896 if i < 3 else 3584)
            going.append(pltpu.make_async_copy(sums.at[:, :, columns], out_ref.at[:, :, columns], out_sems.at[i]))
            going[-1].start()
        for copy in going:
            copy.wait()

    return pl.pallas_call(
        kernel,
        in_specs=[WHOLE] * 4 + [ANY] * (4 + len(after)),
        out_specs=ANY,
        out_shape=jax.ShapeDtypeStruct((4, 32, 6272), half),
        scratch_shapes=[
            pltpu.VMEM((4, 896, 1024), half),
            pltpu.VMEM((4, 32, 6272), half),
            pltpu.SemaphoreType.DMA((4,)),
            pltpu.SemaphoreType.DMA((4,)),
        ],
        compiler_params=pltpu.CompilerParams(vmem_limit_bytes=LIMIT),
        cost_estimate=COST,
    )(*pieces, *weights, *after)


def act(gate, up):
    return (gate / (1.0 + jnp.exp(-gate)) * up).astype(half)


def block(sums, i):
    at = 896 * i
    return act(sums[:, at : at + 448], sums[:, at + 448 : at + 896])


def activate_early(sums, after):
    rows = sums.shape[1]

    def kernel(sums_ref, *refs):
        out_ref = refs[-1]
        total = jnp.sum(sums_ref[...].astype(wide), axis=0)
        out_ref[...] = jnp.concatenate([block(total, i) for i in range(3)], axis=1)

    return pl.pallas_call(
        kernel,
        grid=(1,),
        in_specs=[pl.BlockSpec((4, rows, 2688), lambda i: (0, 0, 0))] + [ANY] * len(after),
        out_specs=pl.BlockSpec((rows, 1344), lambda i: (0, 0)),
        out_shape=jax.ShapeDtypeStruct((rows, 1344), half),
        compiler_params=pltpu.CompilerParams(vmem_limit_bytes=LIMIT),
        cost_estimate=COST,
    )(sums, *after)


def activate_late(sums, near, own, after):
    def kernel(sums_ref, near_ref, own_ref, *refs):
        outs = refs[-3:]
        total = jnp.sum(sums_ref[...].astype(wide), axis=0)
        blocks = [block(total, i) for i in range(7)]
        far = jnp.concatenate(blocks[:4], axis=1)
        near = jnp.concatenate([near_ref[...], jnp.concatenate(blocks[4:6])], axis=1)
        own = jnp.concatenate([own_ref[...], blocks[6]], axis=1)
        for part, out in zip((far, near, own), outs):
            for j in range(4):
                out[j] = part

    return pl.pallas_call(
        kernel,
        grid=(1,),
        in_specs=[
            pl.BlockSpec((4, 32, 6272), lambda i: (0, 0, 0)),
            pl.BlockSpec((64, 1344), lambda i: (0, 0)),
            pl.BlockSpec((32, 1344), lambda i: (0, 0)),
        ]
        + [ANY] * len(after),
        out_specs=[pl.BlockSpec((4, r, 1792), lambda i: (0, 0, 0)) for r in (32, 64, 32)],
        out_shape=[jax.ShapeDtypeStruct((4, r, 1792), half) for r in (32, 64, 32)],
        compiler_params=pltpu.CompilerParams(vmem_limit_bytes=LIMIT),
        cost_estimate=COST,
    )(sums, near, own, *after)


def down(hidden, weights, types):
    n = len(types)

    def kernel(*refs):
        hidden_ref, v_refs, outs = refs[0], refs[1:5], refs[5:]
        v = jnp.concatenate([ref[...] for ref in v_refs])
        for i, out in enumerate(outs):
            rows = hidden_ref[:, pl.ds(32 * i, 32), :].reshape(128, 1792)
            out[...] = jnp.dot(rows, v, preferred_element_type=wide).astype(out.dtype)

    return pl.pallas_call(
        kernel,
        grid=(2,),
        in_specs=[pl.BlockSpec((4, 32 * n, 1792), lambda i: (0, 0, 0))]
        + [pl.BlockSpec((448, 512), lambda i: (0, i))] * 4,
        out_specs=[pl.BlockSpec((128, 512), lambda i: (0, i))] * n,
        out_shape=[jax.ShapeDtypeStruct((128, 1024), t) for t in types],
        compiler_params=pltpu.CompilerParams(vmem_limit_bytes=LIMIT),
        cost_estimate=COST,
    )(hidden, *weights)


def on_device(tokens, routes, route_gates, w_in, w_down):
    core = lax.axis_index("core")
    zlo = lax.axis_index("zlo")
    expert = zlo * 2 + core

    mine = [tokens[0]] + [shift(tokens[0], "zlo", d) for d in (1, 2, 3)]
    w_own, v_own = jnp.transpose(w_in[0], (1, 2, 0)).reshape(896, 1024), w_down[0]
    w_first, w_second = pass_on(w_own, "y", 1), pass_on(w_own, "y", -1)
    v_first, v_second = pass_on(v_own, "y", 1), pass_on(v_own, "y", -1)
    weights = [w_own, w_first, w_second]

    matches = routes[:, :, None] == jnp.arange(8, dtype=jnp.int32)[None, None, :]
    hit = jnp.sum(matches.astype(jnp.int32), axis=1)
    slot = jnp.cumsum(hit, axis=0) - hit
    weight = jnp.sum(route_gates[:, :, None] * matches.astype(wide), axis=1)
    names = jnp.arange(8, dtype=jnp.int32)

    def places(e):
        taken = lax.dynamic_index_in_dim(hit, e, 1, keepdims=False)
        place = lax.dynamic_index_in_dim(slot, e, 1, keepdims=False)
        chosen = [(taken == 1) & (place == k) for k in range(2)]
        owner = [jnp.sum(jnp.where(c, names >> 1, 0)) for c in chosen]
        side = [jnp.sum(jnp.where(c, names & 1, 0)) for c in chosen]
        return chosen, owner, side

    chosen, owner, side = places(expert)
    _, owner_too, _ = places(expert + 1 - 2 * core)
    gates = lax.dynamic_index_in_dim(weight, expert, 1, keepdims=False)
    scales = [jnp.sum(jnp.where(c, gates, 0.0)) for c in chosen]

    def taking(owners):
        out = []
        for z in owners:
            away = (zlo - z) & 3
            near = jnp.where(away == 0, mine[0], mine[1])
            out.append(jnp.where(away < 2, near, jnp.where(away == 2, mine[2], mine[3])))
        return out

    other = shift(jnp.concatenate(taking(owner_too)), "core", 1)
    rows = jnp.concatenate(
        [jnp.where(side[k] == core, a, other[64 * k : 64 * k + 64]) for k, a in enumerate(taking(owner))]
    )

    first, second = pass_on(rows, "zhi", 1), pass_on(rows, "zhi", -1)
    w_next, own_part = early([rows], weights, True, [])
    own_sums = swap(own_part, "x")
    w_far = pass_on(w_next, "y", 1)

    (part,) = early([first, second], weights, False, [own_part])
    far = pass_on(first, "zhi", 1)
    v_far = pass_on(v_first, "y", 1)
    v_all = [v_own, v_first, v_second, v_far]
    own_h, near_h = activate_early(own_sums, []), activate_early(swap(part, "x"), [v_first])
    rest = swap(late([far, first, second, rows], weights + [w_far], []), "x")
    far_h, near_h, own_h = activate_late(rest, near_h, own_h, [v_second, v_far])

    (far_out,) = down(swap(far_h, "x"), v_all, (half,))
    got = pass_on(far_out, "zhi", 1)
    first_out, second_out = down(swap(near_h, "x"), v_all, (half, wide))
    back = pass_on(first_out, "zhi", -1)
    ahead = pass_on((second_out + got.astype(wide)).astype(half), "zhi", 1)

    (own_out,) = down(swap(own_h, "x"), v_all, (wide,))
    result = (own_out + ahead.astype(wide) + back.astype(wide)).reshape(2, 64, 1024)

    ids = jnp.arange(4, dtype=jnp.int32)[:, None, None]

    def toward(parity):
        return sum(
            jnp.where((owner[k] == ids) & (side[k] == parity), scales[k] * result[k][None], 0.0)
            for k in range(2)
        )

    got = shift(toward(1 - core).astype(half), "core", 1)
    going = (toward(core) + got.astype(wide)).astype(half)
    return jnp.sum(swap(going, "zlo").astype(wide), axis=0, keepdims=True).astype(half)


def solution(mesh):
    fine = Mesh(mesh.devices.reshape(4, 2, 4, 4, 4), ("zlo", "core", "x", "y", "zhi"))
    seqs, pos = ("zlo", "core"), ("y", "zhi")
    return jax.shard_map(
        on_device,
        mesh=fine,
        in_specs=(
            P(seqs, pos, "x"),
            P(),
            P(),
            P(seqs, "x", None, pos),
            P(seqs, pos, "x"),
        ),
        out_specs=P(seqs, pos, "x"),
        check_vma=False,
    )
```

```python
import jax
import jax.numpy as jnp
from jax import lax
from jax.experimental import pallas as pl
from jax.experimental.pallas import tpu as pltpu
from jax.sharding import Mesh, PartitionSpec as P

wide = jnp.float32
half = jnp.bfloat16
LIMIT = 60 * 2**20
SOME = pl.CostEstimate(flops=10 * 10**9, bytes_accessed=1024, transcendentals=0)
LONG = pl.CostEstimate(flops=10**11, bytes_accessed=1024, transcendentals=0)
COST = pl.CostEstimate(flops=1024, bytes_accessed=1024, transcendentals=0)
ANY = pl.BlockSpec(memory_space=pl.ANY)
WHOLE = pl.BlockSpec(memory_space=pltpu.VMEM)


def shift(a, axis, by):
    n = lax.axis_size(axis)
    return lax.ppermute(a, axis, [(i, (i + by) % n) for i in range(n)])


def pass_on(a, axis, by):
    n = lax.axis_size(axis)
    return lax.ppermute(
        a, ("core", axis), [(c * n + i, c * n + (i + by * (1 - 2 * c)) % n) for c in range(2) for i in range(n)]
    )


def swap(a, axis):
    return lax.all_to_all(a, axis, split_axis=0, concat_axis=0, tiled=True)


DIMS = (((1,), (1,)), ((), ()))


def hold(a, after, cost):
    def kernel(a_ref, *refs):
        refs[-1][...] = a_ref[...]

    return pl.pallas_call(
        kernel,
        in_specs=[WHOLE] + [ANY] * len(after),
        out_specs=WHOLE,
        out_shape=jax.ShapeDtypeStruct(a.shape, a.dtype),
        compiler_params=pltpu.CompilerParams(vmem_limit_bytes=LIMIT),
        cost_estimate=cost,
    )(a, *after)


def fetch(refs, held, sems):
    copies = [pltpu.make_async_copy(ref, held.at[i], sems.at[i]) for i, ref in enumerate(refs)]
    for copy in copies:
        copy.start()
    return copies


def early(pieces, weights, spare, after):
    n = len(pieces)

    def kernel(*refs):
        out_ref, held, sums, sems, out_sems = refs[-5:]
        copies = fetch(refs[n : n + 3], held, sems)
        x = jnp.concatenate([ref[...] for ref in refs[:n]])
        going = []
        for i in range(3):
            copies[i].wait()
            if i == 1 and spare:
                going.append(pltpu.make_async_copy(held.at[1], refs[-6], out_sems.at[3]))
                going[-1].start()
            columns = pl.ds(896 * i, 896)
            out = lax.dot_general(x, held[i], DIMS, preferred_element_type=wide).astype(half)
            for p in range(n):
                sums[:, pl.ds(32 * p, 32), columns] = out[128 * p : 128 * p + 128].reshape(4, 32, 896)
            going.append(pltpu.make_async_copy(sums.at[:, :, columns], out_ref.at[:, :, columns], out_sems.at[i]))
            going[-1].start()
        for copy in going:
            copy.wait()

    shapes = [(896, 1024)] * spare + [(4, 32 * n, 2688)]
    return pl.pallas_call(
        kernel,
        in_specs=[WHOLE] * n + [ANY] * (3 + len(after)),
        out_specs=[ANY] * len(shapes),
        out_shape=[jax.ShapeDtypeStruct(shape, half) for shape in shapes],
        scratch_shapes=[
            pltpu.VMEM((3, 896, 1024), half),
            pltpu.VMEM((4, 32 * n, 2688), half),
            pltpu.SemaphoreType.DMA((3,)),
            pltpu.SemaphoreType.DMA((4,)),
        ],
        compiler_params=pltpu.CompilerParams(vmem_limit_bytes=LIMIT),
        cost_estimate=LONG if spare else SOME,
    )(*pieces, *weights, *after)


def late(pieces, weights, after):
    def kernel(*refs):
        out_ref, held, sums, sems, out_sems = refs[-5:]
        copies = fetch(refs[4:8], held, sems)
        x = jnp.concatenate([ref[...] for ref in refs[:4]])
        going = []
        for i in range(4):
            copies[i].wait()
            rows = x[:128] if i < 3 else x
            out = lax.dot_general(rows, held[i], DIMS, preferred_element_type=wide).astype(half)
            for p in range(1 if i < 3 else 4):
                columns = pl.ds(896 * (i + p), 896)
                sums[:, :, columns] = out[128 * p : 128 * p + 128].reshape(4, 32, 896)
            columns = pl.ds(896 * i, 896 if i < 3 else 3584)
            going.append(pltpu.make_async_copy(sums.at[:, :, columns], out_ref.at[:, :, columns], out_sems.at[i]))
            going[-1].start()
        for copy in going:
            copy.wait()

    return pl.pallas_call(
        kernel,
        in_specs=[WHOLE] * 4 + [ANY] * (4 + len(after)),
        out_specs=ANY,
        out_shape=jax.ShapeDtypeStruct((4, 32, 6272), half),
        scratch_shapes=[
            pltpu.VMEM((4, 896, 1024), half),
            pltpu.VMEM((4, 32, 6272), half),
            pltpu.SemaphoreType.DMA((4,)),
            pltpu.SemaphoreType.DMA((4,)),
        ],
        compiler_params=pltpu.CompilerParams(vmem_limit_bytes=LIMIT),
        cost_estimate=LONG,
    )(*pieces, *weights, *after)


def act(gate, up):
    return (gate / (1.0 + jnp.exp(-gate)) * up).astype(half)


def block(sums, i):
    at = 896 * i
    return act(sums[:, at : at + 448], sums[:, at + 448 : at + 896])


def activate_early(sums, after):
    rows = sums.shape[1]

    def kernel(sums_ref, *refs):
        out_ref = refs[-1]
        total = jnp.sum(sums_ref[...].astype(wide), axis=0)
        out_ref[...] = jnp.concatenate([block(total, i) for i in range(3)], axis=1)

    return pl.pallas_call(
        kernel,
        grid=(1,),
        in_specs=[pl.BlockSpec((4, rows, 2688), lambda i: (0, 0, 0))] + [ANY] * len(after),
        out_specs=pl.BlockSpec((rows, 1344), lambda i: (0, 0)),
        out_shape=jax.ShapeDtypeStruct((rows, 1344), half),
        compiler_params=pltpu.CompilerParams(vmem_limit_bytes=LIMIT),
        cost_estimate=COST,
    )(sums, *after)


def activate_late(sums, near, own, after):
    def kernel(sums_ref, near_ref, own_ref, *refs):
        outs = refs[-3:]
        total = jnp.sum(sums_ref[...].astype(wide), axis=0)
        blocks = [block(total, i) for i in range(7)]
        far = jnp.concatenate(blocks[:4], axis=1)
        near = jnp.concatenate([near_ref[...], jnp.concatenate(blocks[4:6])], axis=1)
        own = jnp.concatenate([own_ref[...], blocks[6]], axis=1)
        for part, out in zip((far, near, own), outs):
            for j in range(4):
                out[j] = part

    return pl.pallas_call(
        kernel,
        grid=(1,),
        in_specs=[
            pl.BlockSpec((4, 32, 6272), lambda i: (0, 0, 0)),
            pl.BlockSpec((64, 1344), lambda i: (0, 0)),
            pl.BlockSpec((32, 1344), lambda i: (0, 0)),
        ]
        + [ANY] * len(after),
        out_specs=[pl.BlockSpec((4, r, 1792), lambda i: (0, 0, 0)) for r in (32, 64, 32)],
        out_shape=[jax.ShapeDtypeStruct((4, r, 1792), half) for r in (32, 64, 32)],
        compiler_params=pltpu.CompilerParams(vmem_limit_bytes=LIMIT),
        cost_estimate=COST,
    )(sums, near, own, *after)


def down(hidden, weights, types):
    n = len(types)

    def kernel(*refs):
        hidden_ref, v_refs, outs = refs[0], refs[1:5], refs[5:]
        v = jnp.concatenate([ref[...] for ref in v_refs])
        for i, out in enumerate(outs):
            rows = hidden_ref[:, pl.ds(32 * i, 32), :].reshape(128, 1792)
            out[...] = jnp.dot(rows, v, preferred_element_type=wide).astype(out.dtype)

    return pl.pallas_call(
        kernel,
        grid=(2,),
        in_specs=[pl.BlockSpec((4, 32 * n, 1792), lambda i: (0, 0, 0))]
        + [pl.BlockSpec((448, 512), lambda i: (0, i))] * 4,
        out_specs=[pl.BlockSpec((128, 512), lambda i: (0, i))] * n,
        out_shape=[jax.ShapeDtypeStruct((128, 1024), t) for t in types],
        compiler_params=pltpu.CompilerParams(vmem_limit_bytes=LIMIT),
        cost_estimate=COST,
    )(hidden, *weights)


def on_device(tokens, routes, route_gates, w_in, w_down):
    core = lax.axis_index("core")
    zlo = lax.axis_index("zlo")
    expert = zlo * 2 + core

    mine = [tokens[0]] + [shift(tokens[0], "zlo", d) for d in (1, 2, 3)]
    w_own, v_own = jnp.transpose(w_in[0], (1, 2, 0)).reshape(896, 1024), w_down[0]
    w_first, w_second = pass_on(w_own, "y", 1), pass_on(w_own, "y", -1)
    weights = [w_own, w_first, w_second]

    matches = routes[:, :, None] == jnp.arange(8, dtype=jnp.int32)[None, None, :]
    hit = jnp.sum(matches.astype(jnp.int32), axis=1)
    slot = jnp.cumsum(hit, axis=0) - hit
    weight = jnp.sum(route_gates[:, :, None] * matches.astype(wide), axis=1)
    names = jnp.arange(8, dtype=jnp.int32)

    def places(e):
        taken = lax.dynamic_index_in_dim(hit, e, 1, keepdims=False)
        place = lax.dynamic_index_in_dim(slot, e, 1, keepdims=False)
        chosen = [(taken == 1) & (place == k) for k in range(2)]
        owner = [jnp.sum(jnp.where(c, names >> 1, 0)) for c in chosen]
        side = [jnp.sum(jnp.where(c, names & 1, 0)) for c in chosen]
        return chosen, owner, side

    chosen, owner, side = places(expert)
    _, owner_too, _ = places(expert + 1 - 2 * core)
    gates = lax.dynamic_index_in_dim(weight, expert, 1, keepdims=False)
    scales = [jnp.sum(jnp.where(c, gates, 0.0)) for c in chosen]

    def taking(owners):
        out = []
        for z in owners:
            away = (zlo - z) & 3
            near = jnp.where(away == 0, mine[0], mine[1])
            out.append(jnp.where(away < 2, near, jnp.where(away == 2, mine[2], mine[3])))
        return out

    other = shift(jnp.concatenate(taking(owner_too)), "core", 1)
    rows = jnp.concatenate(
        [jnp.where(side[k] == core, a, other[64 * k : 64 * k + 64]) for k, a in enumerate(taking(owner))]
    )

    first, second = pass_on(rows, "zhi", 1), pass_on(rows, "zhi", -1)
    w_next, own_part = early([rows], weights, True, [])
    own_sums = swap(own_part, "x")
    w_far = pass_on(w_next, "y", 1)

    (part,) = early([first, second], weights, False, [own_part])
    far = pass_on(hold(first, [own_part], SOME), "zhi", 1)
    v_held = hold(v_own, [own_sums], COST)
    v_first, v_second = pass_on(v_held, "y", 1), pass_on(v_held, "y", -1)
    v_far = pass_on(v_first, "y", 1)
    v_all = [v_own, v_first, v_second, v_far]
    own_h, near_h = activate_early(own_sums, []), activate_early(swap(part, "x"), [v_first])
    rest = swap(late([far, first, second, rows], weights + [w_far], []), "x")
    far_h, near_h, own_h = activate_late(rest, near_h, own_h, [v_second, v_far])

    (far_out,) = down(swap(far_h, "x"), v_all, (half,))
    got = pass_on(far_out, "zhi", 1)
    first_out, second_out = down(swap(near_h, "x"), v_all, (half, wide))
    back = pass_on(first_out, "zhi", -1)
    ahead = pass_on((second_out + got.astype(wide)).astype(half), "zhi", 1)

    (own_out,) = down(swap(own_h, "x"), v_all, (wide,))
    result = (own_out + ahead.astype(wide) + back.astype(wide)).reshape(2, 64, 1024)

    ids = jnp.arange(4, dtype=jnp.int32)[:, None, None]

    def toward(parity):
        return sum(
            jnp.where((owner[k] == ids) & (side[k] == parity), scales[k] * result[k][None], 0.0)
            for k in range(2)
        )

    got = shift(toward(1 - core).astype(half), "core", 1)
    going = (toward(core) + got.astype(wide)).astype(half)
    return jnp.sum(swap(going, "zlo").astype(wide), axis=0, keepdims=True).astype(half)


def solution(mesh):
    fine = Mesh(mesh.devices.reshape(4, 2, 4, 4, 4), ("zlo", "core", "x", "y", "zhi"))
    seqs, pos = ("zlo", "core"), ("y", "zhi")
    return jax.shard_map(
        on_device,
        mesh=fine,
        in_specs=(
            P(seqs, pos, "x"),
            P(),
            P(),
            P(seqs, "x", None, pos),
            P(seqs, pos, "x"),
        ),
        out_specs=P(seqs, pos, "x"),
        check_vma=False,
    )
```

```python
import jax
import jax.numpy as jnp
from jax import lax
from jax.experimental import pallas as pl
from jax.experimental.pallas import tpu as pltpu
from jax.sharding import Mesh, PartitionSpec as P

wide = jnp.float32
half = jnp.bfloat16
LIMIT = 60 * 2**20
SOME = pl.CostEstimate(flops=10 * 10**9, bytes_accessed=1024, transcendentals=0)
LONG = pl.CostEstimate(flops=10**11, bytes_accessed=1024, transcendentals=0)
COST = pl.CostEstimate(flops=1024, bytes_accessed=1024, transcendentals=0)
ANY = pl.BlockSpec(memory_space=pl.ANY)
WHOLE = pl.BlockSpec(memory_space=pltpu.VMEM)


def shift(a, axis, by):
    n = lax.axis_size(axis)
    return lax.ppermute(a, axis, [(i, (i + by) % n) for i in range(n)])


def pass_on(a, axis, by):
    n = lax.axis_size(axis)
    return lax.ppermute(
        a, ("core", axis), [(c * n + i, c * n + (i + by * (1 - 2 * c)) % n) for c in range(2) for i in range(n)]
    )


def swap(a, axis):
    return lax.all_to_all(a, axis, split_axis=0, concat_axis=0, tiled=True)


DIMS = (((1,), (1,)), ((), ()))


def hold(a, after, cost):
    def kernel(a_ref, *refs):
        refs[-1][...] = a_ref[...]

    return pl.pallas_call(
        kernel,
        in_specs=[WHOLE] + [ANY] * len(after),
        out_specs=WHOLE,
        out_shape=jax.ShapeDtypeStruct(a.shape, a.dtype),
        compiler_params=pltpu.CompilerParams(vmem_limit_bytes=LIMIT),
        cost_estimate=cost,
    )(a, *after)


def fetch(refs, held, sems):
    copies = [pltpu.make_async_copy(ref, held.at[i], sems.at[i]) for i, ref in enumerate(refs)]
    for copy in copies:
        copy.start()
    return copies


def early(pieces, weights, spare, after):
    n = len(pieces)

    def kernel(*refs):
        out_ref, held, sums, sems, out_sems = refs[-5:]
        copies = fetch(refs[n : n + 3], held, sems)
        x = jnp.concatenate([ref[...] for ref in refs[:n]])
        going = []
        for i in range(3):
            copies[i].wait()
            if i == 1 and spare:
                going.append(pltpu.make_async_copy(held.at[1], refs[-6], out_sems.at[3]))
                going[-1].start()
            columns = pl.ds(896 * i, 896)
            out = lax.dot_general(x, held[i], DIMS, preferred_element_type=wide).astype(half)
            for p in range(n):
                sums[:, pl.ds(32 * p, 32), columns] = out[128 * p : 128 * p + 128].reshape(4, 32, 896)
            going.append(pltpu.make_async_copy(sums.at[:, :, columns], out_ref.at[:, :, columns], out_sems.at[i]))
            going[-1].start()
        for copy in going:
            copy.wait()

    shapes = [(896, 1024)] * spare + [(4, 32 * n, 2688)]
    return pl.pallas_call(
        kernel,
        in_specs=[WHOLE] * n + [ANY] * (3 + len(after)),
        out_specs=[ANY] * len(shapes),
        out_shape=[jax.ShapeDtypeStruct(shape, half) for shape in shapes],
        scratch_shapes=[
            pltpu.VMEM((3, 896, 1024), half),
            pltpu.VMEM((4, 32 * n, 2688), half),
            pltpu.SemaphoreType.DMA((3,)),
            pltpu.SemaphoreType.DMA((4,)),
        ],
        compiler_params=pltpu.CompilerParams(vmem_limit_bytes=LIMIT),
        cost_estimate=LONG if spare else SOME,
    )(*pieces, *weights, *after)


def late_far(far, weights):
    def kernel(far_ref, *refs):
        out_ref, held, sums, sems, out_sems = refs[-5:]
        copies = fetch(refs[:4], held, sems)
        going = []
        for i in range(4):
            copies[i].wait()
            columns = pl.ds(896 * i, 896)
            out = lax.dot_general(far_ref[...], held[i], DIMS, preferred_element_type=wide).astype(half)
            sums[:, :, columns] = out.reshape(4, 32, 896)
            going.append(pltpu.make_async_copy(sums.at[:, :, columns], out_ref.at[:, :, columns], out_sems.at[i]))
            going[-1].start()
        for copy in going:
            copy.wait()

    return pl.pallas_call(
        kernel,
        in_specs=[WHOLE] + [ANY] * 4,
        out_specs=ANY,
        out_shape=jax.ShapeDtypeStruct((4, 32, 3584), half),
        scratch_shapes=[
            pltpu.VMEM((4, 896, 1024), half),
            pltpu.VMEM((4, 32, 3584), half),
            pltpu.SemaphoreType.DMA((4,)),
            pltpu.SemaphoreType.DMA((4,)),
        ],
        compiler_params=pltpu.CompilerParams(vmem_limit_bytes=LIMIT),
        cost_estimate=LONG,
    )(far, *weights)


def late_rest(pieces, w_far, after):
    def kernel(*refs):
        out_ref = refs[-1]
        x = jnp.concatenate([ref[...] for ref in refs[:3]])
        out = lax.dot_general(x, refs[3][...], DIMS, preferred_element_type=wide).astype(half)
        for p in range(3):
            out_ref[:, :, pl.ds(896 * p, 896)] = out[128 * p : 128 * p + 128].reshape(4, 32, 896)

    return pl.pallas_call(
        kernel,
        in_specs=[WHOLE] * 4 + [ANY] * len(after),
        out_specs=WHOLE,
        out_shape=jax.ShapeDtypeStruct((4, 32, 2688), half),
        compiler_params=pltpu.CompilerParams(vmem_limit_bytes=LIMIT),
        cost_estimate=COST,
    )(*pieces, w_far, *after)


def act(gate, up):
    return (gate / (1.0 + jnp.exp(-gate)) * up).astype(half)


def block(sums, i):
    at = 896 * i
    return act(sums[:, at : at + 448], sums[:, at + 448 : at + 896])


def activate_early(sums, after):
    rows = sums.shape[1]

    def kernel(sums_ref, *refs):
        out_ref = refs[-1]
        total = jnp.sum(sums_ref[...].astype(wide), axis=0)
        out_ref[...] = jnp.concatenate([block(total, i) for i in range(3)], axis=1)

    return pl.pallas_call(
        kernel,
        grid=(1,),
        in_specs=[pl.BlockSpec((4, rows, 2688), lambda i: (0, 0, 0))] + [ANY] * len(after),
        out_specs=pl.BlockSpec((rows, 1344), lambda i: (0, 0)),
        out_shape=jax.ShapeDtypeStruct((rows, 1344), half),
        compiler_params=pltpu.CompilerParams(vmem_limit_bytes=LIMIT),
        cost_estimate=COST,
    )(sums, *after)


def activate_far(sums):
    def kernel(sums_ref, out_ref):
        total = jnp.sum(sums_ref[...].astype(wide), axis=0)
        hidden = jnp.concatenate([block(total, i) for i in range(4)], axis=1)
        for j in range(4):
            out_ref[j] = hidden

    return pl.pallas_call(
        kernel,
        grid=(1,),
        in_specs=[pl.BlockSpec((4, 32, 3584), lambda i: (0, 0, 0))],
        out_specs=pl.BlockSpec((4, 32, 1792), lambda i: (0, 0, 0)),
        out_shape=jax.ShapeDtypeStruct((4, 32, 1792), half),
        compiler_params=pltpu.CompilerParams(vmem_limit_bytes=LIMIT),
        cost_estimate=COST,
    )(sums)


def activate_rest(sums, near, own, after):
    def kernel(sums_ref, near_ref, own_ref, *refs):
        outs = refs[-2:]
        total = jnp.sum(sums_ref[...].astype(wide), axis=0)
        blocks = [block(total, i) for i in range(3)]
        near = jnp.concatenate([near_ref[...], jnp.concatenate(blocks[:2])], axis=1)
        own = jnp.concatenate([own_ref[...], blocks[2]], axis=1)
        for part, out in zip((near, own), outs):
            for j in range(4):
                out[j] = part

    return pl.pallas_call(
        kernel,
        grid=(1,),
        in_specs=[
            pl.BlockSpec((4, 32, 2688), lambda i: (0, 0, 0)),
            pl.BlockSpec((64, 1344), lambda i: (0, 0)),
            pl.BlockSpec((32, 1344), lambda i: (0, 0)),
        ]
        + [ANY] * len(after),
        out_specs=[pl.BlockSpec((4, r, 1792), lambda i: (0, 0, 0)) for r in (64, 32)],
        out_shape=[jax.ShapeDtypeStruct((4, r, 1792), half) for r in (64, 32)],
        compiler_params=pltpu.CompilerParams(vmem_limit_bytes=LIMIT),
        cost_estimate=COST,
    )(sums, near, own, *after)


def down(hidden, weights, types):
    n = len(types)

    def kernel(*refs):
        hidden_ref, v_refs, outs = refs[0], refs[1:5], refs[5:]
        v = jnp.concatenate([ref[...] for ref in v_refs])
        for i, out in enumerate(outs):
            rows = hidden_ref[:, pl.ds(32 * i, 32), :].reshape(128, 1792)
            out[...] = jnp.dot(rows, v, preferred_element_type=wide).astype(out.dtype)

    return pl.pallas_call(
        kernel,
        grid=(2,),
        in_specs=[pl.BlockSpec((4, 32 * n, 1792), lambda i: (0, 0, 0))]
        + [pl.BlockSpec((448, 512), lambda i: (0, i))] * 4,
        out_specs=[pl.BlockSpec((128, 512), lambda i: (0, i))] * n,
        out_shape=[jax.ShapeDtypeStruct((128, 1024), t) for t in types],
        compiler_params=pltpu.CompilerParams(vmem_limit_bytes=LIMIT),
        cost_estimate=COST,
    )(hidden, *weights)


def on_device(tokens, routes, route_gates, w_in, w_down):
    core = lax.axis_index("core")
    zlo = lax.axis_index("zlo")
    expert = zlo * 2 + core

    mine = [tokens[0]] + [shift(tokens[0], "zlo", d) for d in (1, 2, 3)]
    w_own, v_own = jnp.transpose(w_in[0], (1, 2, 0)).reshape(896, 1024), w_down[0]
    w_first, w_second = pass_on(w_own, "y", 1), pass_on(w_own, "y", -1)
    weights = [w_own, w_first, w_second]

    matches = routes[:, :, None] == jnp.arange(8, dtype=jnp.int32)[None, None, :]
    hit = jnp.sum(matches.astype(jnp.int32), axis=1)
    slot = jnp.cumsum(hit, axis=0) - hit
    weight = jnp.sum(route_gates[:, :, None] * matches.astype(wide), axis=1)
    names = jnp.arange(8, dtype=jnp.int32)

    def places(e):
        taken = lax.dynamic_index_in_dim(hit, e, 1, keepdims=False)
        place = lax.dynamic_index_in_dim(slot, e, 1, keepdims=False)
        chosen = [(taken == 1) & (place == k) for k in range(2)]
        owner = [jnp.sum(jnp.where(c, names >> 1, 0)) for c in chosen]
        side = [jnp.sum(jnp.where(c, names & 1, 0)) for c in chosen]
        return chosen, owner, side

    chosen, owner, side = places(expert)
    _, owner_too, _ = places(expert + 1 - 2 * core)
    gates = lax.dynamic_index_in_dim(weight, expert, 1, keepdims=False)
    scales = [jnp.sum(jnp.where(c, gates, 0.0)) for c in chosen]

    def taking(owners):
        out = []
        for z in owners:
            away = (zlo - z) & 3
            near = jnp.where(away == 0, mine[0], mine[1])
            out.append(jnp.where(away < 2, near, jnp.where(away == 2, mine[2], mine[3])))
        return out

    other = shift(jnp.concatenate(taking(owner_too)), "core", 1)
    rows = jnp.concatenate(
        [jnp.where(side[k] == core, a, other[64 * k : 64 * k + 64]) for k, a in enumerate(taking(owner))]
    )

    first, second = pass_on(rows, "zhi", 1), pass_on(rows, "zhi", -1)
    w_next, own_part = early([rows], weights, True, [])
    own_sums = swap(own_part, "x")
    w_far = pass_on(w_next, "y", 1)

    (part,) = early([first, second], weights, False, [own_part])
    far = pass_on(hold(first, [own_part], SOME), "zhi", 1)
    v_held = hold(v_own, [own_sums], COST)
    v_first, v_second = pass_on(v_held, "y", 1), pass_on(v_held, "y", -1)
    v_far = pass_on(v_first, "y", 1)
    v_all = [v_own, v_first, v_second, v_far]
    own_h, near_h = activate_early(own_sums, []), activate_early(swap(part, "x"), [v_first])
    far_part = late_far(far, weights + [w_far])
    rest_part = late_rest([first, second, rows], w_far, [far_part])
    far_h = activate_far(swap(far_part, "x"))
    near_h, own_h = activate_rest(swap(rest_part, "x"), near_h, own_h, [v_second, v_far])

    (far_out,) = down(swap(far_h, "x"), v_all, (half,))
    got = pass_on(far_out, "zhi", 1)
    first_out, second_out = down(swap(near_h, "x"), v_all, (half, wide))
    back = pass_on(first_out, "zhi", -1)
    ahead = pass_on((second_out + got.astype(wide)).astype(half), "zhi", 1)

    (own_out,) = down(swap(own_h, "x"), v_all, (wide,))
    result = (own_out + ahead.astype(wide) + back.astype(wide)).reshape(2, 64, 1024)

    ids = jnp.arange(4, dtype=jnp.int32)[:, None, None]

    def toward(parity):
        return sum(
            jnp.where((owner[k] == ids) & (side[k] == parity), scales[k] * result[k][None], 0.0)
            for k in range(2)
        )

    got = shift(toward(1 - core).astype(half), "core", 1)
    going = (toward(core) + got.astype(wide)).astype(half)
    return jnp.sum(swap(going, "zlo").astype(wide), axis=0, keepdims=True).astype(half)


def solution(mesh):
    fine = Mesh(mesh.devices.reshape(4, 2, 4, 4, 4), ("zlo", "core", "x", "y", "zhi"))
    seqs, pos = ("zlo", "core"), ("y", "zhi")
    return jax.shard_map(
        on_device,
        mesh=fine,
        in_specs=(
            P(seqs, pos, "x"),
            P(),
            P(),
            P(seqs, "x", None, pos),
            P(seqs, pos, "x"),
        ),
        out_specs=P(seqs, pos, "x"),
        check_vma=False,
    )
```

```python
import jax
import jax.numpy as jnp
from jax import lax
from jax.experimental import pallas as pl
from jax.experimental.pallas import tpu as pltpu
from jax.sharding import Mesh, PartitionSpec as P

wide = jnp.float32
half = jnp.bfloat16
LIMIT = 60 * 2**20
SOME = pl.CostEstimate(flops=10 * 10**9, bytes_accessed=1024, transcendentals=0)
LONG = pl.CostEstimate(flops=10**11, bytes_accessed=1024, transcendentals=0)
COST = pl.CostEstimate(flops=1024, bytes_accessed=1024, transcendentals=0)
ANY = pl.BlockSpec(memory_space=pl.ANY)
WHOLE = pl.BlockSpec(memory_space=pltpu.VMEM)


def shift(a, axis, by):
    n = lax.axis_size(axis)
    return lax.ppermute(a, axis, [(i, (i + by) % n) for i in range(n)])


def pass_on(a, axis, by):
    n = lax.axis_size(axis)
    return lax.ppermute(
        a, ("core", axis), [(c * n + i, c * n + (i + by * (1 - 2 * c)) % n) for c in range(2) for i in range(n)]
    )


def swap(a, axis):
    return lax.all_to_all(a, axis, split_axis=0, concat_axis=0, tiled=True)


DIMS = (((1,), (1,)), ((), ()))


def hold(a, after, cost):
    def kernel(a_ref, *refs):
        refs[-1][...] = a_ref[...]

    return pl.pallas_call(
        kernel,
        in_specs=[WHOLE] + [ANY] * len(after),
        out_specs=WHOLE,
        out_shape=jax.ShapeDtypeStruct(a.shape, a.dtype),
        compiler_params=pltpu.CompilerParams(vmem_limit_bytes=LIMIT),
        cost_estimate=cost,
    )(a, *after)


def fetch(refs, held, sems):
    copies = [pltpu.make_async_copy(ref, held.at[i], sems.at[i]) for i, ref in enumerate(refs)]
    for copy in copies:
        copy.start()
    return copies


def early(pieces, weights, spare, after):
    n = len(pieces)

    def kernel(*refs):
        out_ref, held, sums, sems, out_sems = refs[-5:]
        copies = fetch(refs[n : n + 3], held, sems)
        x = jnp.concatenate([ref[...] for ref in refs[:n]])
        going = []
        for i in range(3):
            copies[i].wait()
            if i == 1 and spare:
                going.append(pltpu.make_async_copy(held.at[1], refs[-6], out_sems.at[3]))
                going[-1].start()
            columns = pl.ds(896 * i, 896)
            out = lax.dot_general(x, held[i], DIMS, preferred_element_type=wide).astype(half)
            for p in range(n):
                sums[:, pl.ds(32 * p, 32), columns] = out[128 * p : 128 * p + 128].reshape(4, 32, 896)
            going.append(pltpu.make_async_copy(sums.at[:, :, columns], out_ref.at[:, :, columns], out_sems.at[i]))
            going[-1].start()
        for copy in going:
            copy.wait()

    shapes = [(896, 1024)] * spare + [(4, 32 * n, 2688)]
    return pl.pallas_call(
        kernel,
        in_specs=[WHOLE] * n + [ANY] * (3 + len(after)),
        out_specs=[ANY] * len(shapes),
        out_shape=[jax.ShapeDtypeStruct(shape, half) for shape in shapes],
        scratch_shapes=[
            pltpu.VMEM((3, 896, 1024), half),
            pltpu.VMEM((4, 32 * n, 2688), half),
            pltpu.SemaphoreType.DMA((3,)),
            pltpu.SemaphoreType.DMA((4,)),
        ],
        compiler_params=pltpu.CompilerParams(vmem_limit_bytes=LIMIT),
        cost_estimate=LONG if spare else SOME,
    )(*pieces, *weights, *after)


def late_far(far, weights):
    def kernel(far_ref, *refs):
        out_ref, held, sums, sems, out_sems = refs[-5:]
        copies = fetch(refs[:4], held, sems)
        going = []
        for i in range(4):
            copies[i].wait()
            columns = pl.ds(896 * i, 896)
            out = lax.dot_general(far_ref[...], held[i], DIMS, preferred_element_type=wide).astype(half)
            sums[:, :, columns] = out.reshape(4, 32, 896)
            going.append(pltpu.make_async_copy(sums.at[:, :, columns], out_ref.at[:, :, columns], out_sems.at[i]))
            going[-1].start()
        for copy in going:
            copy.wait()

    return pl.pallas_call(
        kernel,
        in_specs=[WHOLE] + [ANY] * 4,
        out_specs=ANY,
        out_shape=jax.ShapeDtypeStruct((4, 32, 3584), half),
        scratch_shapes=[
            pltpu.VMEM((4, 896, 1024), half),
            pltpu.VMEM((4, 32, 3584), half),
            pltpu.SemaphoreType.DMA((4,)),
            pltpu.SemaphoreType.DMA((4,)),
        ],
        compiler_params=pltpu.CompilerParams(vmem_limit_bytes=LIMIT),
        cost_estimate=LONG,
    )(far, *weights)


def late_rest(pieces, w_far, after):
    def kernel(*refs):
        out_ref = refs[-1]
        x = jnp.concatenate([ref[...] for ref in refs[:3]])
        out = lax.dot_general(x, refs[3][...], DIMS, preferred_element_type=wide).astype(half)
        for p in range(3):
            out_ref[:, :, pl.ds(896 * p, 896)] = out[128 * p : 128 * p + 128].reshape(4, 32, 896)

    return pl.pallas_call(
        kernel,
        in_specs=[WHOLE] * 4 + [ANY] * len(after),
        out_specs=WHOLE,
        out_shape=jax.ShapeDtypeStruct((4, 32, 2688), half),
        compiler_params=pltpu.CompilerParams(vmem_limit_bytes=LIMIT),
        cost_estimate=COST,
    )(*pieces, w_far, *after)


def act(gate, up):
    return (gate / (1.0 + jnp.exp(-gate)) * up).astype(half)


def block(sums, i):
    at = 896 * i
    return act(sums[:, at : at + 448], sums[:, at + 448 : at + 896])


def activate_early(sums, after):
    rows = sums.shape[1]

    def kernel(sums_ref, *refs):
        out_ref = refs[-1]
        total = jnp.sum(sums_ref[...].astype(wide), axis=0)
        out_ref[...] = jnp.concatenate([block(total, i) for i in range(3)], axis=1)

    return pl.pallas_call(
        kernel,
        grid=(1,),
        in_specs=[pl.BlockSpec((4, rows, 2688), lambda i: (0, 0, 0))] + [ANY] * len(after),
        out_specs=pl.BlockSpec((rows, 1344), lambda i: (0, 0)),
        out_shape=jax.ShapeDtypeStruct((rows, 1344), half),
        compiler_params=pltpu.CompilerParams(vmem_limit_bytes=LIMIT),
        cost_estimate=COST,
    )(sums, *after)


def activate_far(sums):
    def kernel(sums_ref, out_ref):
        total = jnp.sum(sums_ref[...].astype(wide), axis=0)
        out_ref[...] = jnp.concatenate([block(total, i) for i in range(4)], axis=1)

    return pl.pallas_call(
        kernel,
        grid=(1,),
        in_specs=[pl.BlockSpec((4, 32, 3584), lambda i: (0, 0, 0))],
        out_specs=pl.BlockSpec((32, 1792), lambda i: (0, 0)),
        out_shape=jax.ShapeDtypeStruct((32, 1792), half),
        compiler_params=pltpu.CompilerParams(vmem_limit_bytes=LIMIT),
        cost_estimate=LONG,
    )(sums)


def activate_rest(sums, begun, at, after):
    n = begun.shape[0] // 32

    def kernel(sums_ref, begun_ref, *refs):
        total = jnp.sum(sums_ref[:, :, 896 * at : 896 * (at + n)].astype(wide), axis=0)
        blocks = jnp.concatenate([block(total, i) for i in range(n)])
        hidden = jnp.concatenate([begun_ref[...], blocks], axis=1)
        for j in range(4):
            refs[-1][j] = hidden

    return pl.pallas_call(
        kernel,
        grid=(1,),
        in_specs=[
            pl.BlockSpec((4, 32, 2688), lambda i: (0, 0, 0)),
            pl.BlockSpec((32 * n, 1344), lambda i: (0, 0)),
        ]
        + [ANY] * len(after),
        out_specs=pl.BlockSpec((4, 32 * n, 1792), lambda i: (0, 0, 0)),
        out_shape=jax.ShapeDtypeStruct((4, 32 * n, 1792), half),
        compiler_params=pltpu.CompilerParams(vmem_limit_bytes=LIMIT),
        cost_estimate=COST,
    )(sums, begun, *after)


def down(hidden, weights, types):
    n = len(types)

    def kernel(*refs):
        hidden_ref, v_refs, outs = refs[0], refs[1:5], refs[5:]
        v = jnp.concatenate([ref[...] for ref in v_refs])
        for i, out in enumerate(outs):
            rows = hidden_ref[:, pl.ds(32 * i, 32), :].reshape(128, 1792)
            out[...] = jnp.dot(rows, v, preferred_element_type=wide).astype(out.dtype)

    return pl.pallas_call(
        kernel,
        grid=(2,),
        in_specs=[pl.BlockSpec((4, 32 * n, 1792), lambda i: (0, 0, 0))]
        + [pl.BlockSpec((448, 512), lambda i: (0, i))] * 4,
        out_specs=[pl.BlockSpec((128, 512), lambda i: (0, i))] * n,
        out_shape=[jax.ShapeDtypeStruct((128, 1024), t) for t in types],
        compiler_params=pltpu.CompilerParams(vmem_limit_bytes=LIMIT),
        cost_estimate=COST,
    )(hidden, *weights)


def down_far(pieces, weights, x):
    def kernel(x_ref, *refs):
        v_refs, out_ref = refs[4:8], refs[8]
        v = jnp.concatenate([ref[...] for ref in v_refs])
        rows = jnp.concatenate([ref[...] for ref in refs[:4]])
        out = jnp.dot(rows, v, preferred_element_type=wide).astype(half)
        for d in range(4):
            at = pl.multiple_of(((x_ref[0] - d) & 3) * 32, 32)
            out_ref[pl.ds(at, 32), :] = out[32 * d : 32 * d + 32]

    return pl.pallas_call(
        kernel,
        grid=(2,),
        in_specs=[pl.BlockSpec(memory_space=pltpu.SMEM)]
        + [pl.BlockSpec((32, 1792), lambda i: (0, 0))] * 4
        + [pl.BlockSpec((448, 512), lambda i: (0, i))] * 4,
        out_specs=pl.BlockSpec((128, 512), lambda i: (0, i)),
        out_shape=jax.ShapeDtypeStruct((128, 1024), half),
        compiler_params=pltpu.CompilerParams(vmem_limit_bytes=LIMIT),
        cost_estimate=LONG,
    )(x.reshape(1), *pieces, *weights)


def join(a, b):
    def kernel(a_ref, b_ref, out_ref):
        out_ref[...] = (a_ref[...] + b_ref[...].astype(wide)).astype(half)

    return pl.pallas_call(
        kernel,
        in_specs=[WHOLE] * 2,
        out_specs=WHOLE,
        out_shape=jax.ShapeDtypeStruct(a.shape, half),
        compiler_params=pltpu.CompilerParams(vmem_limit_bytes=LIMIT),
        cost_estimate=LONG,
    )(a, b)


def on_device(tokens, routes, route_gates, w_in, w_down):
    core = lax.axis_index("core")
    zlo = lax.axis_index("zlo")
    expert = zlo * 2 + core

    mine = [tokens[0]] + [shift(tokens[0], "zlo", d) for d in (1, 2, 3)]
    w_own, v_own = jnp.transpose(w_in[0], (1, 2, 0)).reshape(896, 1024), w_down[0]
    w_first, w_second = pass_on(w_own, "y", 1), pass_on(w_own, "y", -1)
    weights = [w_own, w_first, w_second]

    matches = routes[:, :, None] == jnp.arange(8, dtype=jnp.int32)[None, None, :]
    hit = jnp.sum(matches.astype(jnp.int32), axis=1)
    slot = jnp.cumsum(hit, axis=0) - hit
    weight = jnp.sum(route_gates[:, :, None] * matches.astype(wide), axis=1)
    names = jnp.arange(8, dtype=jnp.int32)

    def places(e):
        taken = lax.dynamic_index_in_dim(hit, e, 1, keepdims=False)
        place = lax.dynamic_index_in_dim(slot, e, 1, keepdims=False)
        chosen = [(taken == 1) & (place == k) for k in range(2)]
        owner = [jnp.sum(jnp.where(c, names >> 1, 0)) for c in chosen]
        side = [jnp.sum(jnp.where(c, names & 1, 0)) for c in chosen]
        return chosen, owner, side

    chosen, owner, side = places(expert)
    _, owner_too, _ = places(expert + 1 - 2 * core)
    gates = lax.dynamic_index_in_dim(weight, expert, 1, keepdims=False)
    scales = [jnp.sum(jnp.where(c, gates, 0.0)) for c in chosen]

    def taking(owners):
        out = []
        for z in owners:
            away = (zlo - z) & 3
            near = jnp.where(away == 0, mine[0], mine[1])
            out.append(jnp.where(away < 2, near, jnp.where(away == 2, mine[2], mine[3])))
        return out

    other = shift(jnp.concatenate(taking(owner_too)), "core", 1)
    rows = jnp.concatenate(
        [jnp.where(side[k] == core, a, other[64 * k : 64 * k + 64]) for k, a in enumerate(taking(owner))]
    )

    first, second = pass_on(rows, "zhi", 1), pass_on(rows, "zhi", -1)
    w_next, own_part = early([rows], weights, True, [])
    own_sums = swap(own_part, "x")
    w_far = pass_on(w_next, "y", 1)

    (part,) = early([first, second], weights, False, [own_part])
    far = pass_on(hold(first, [own_part], SOME), "zhi", 1)
    v_held = hold(v_own, [own_sums], COST)
    v_first, v_second = pass_on(v_held, "y", 1), pass_on(v_held, "y", -1)
    v_far = pass_on(v_first, "y", 1)
    v_all = [v_own, v_first, v_second, v_far]
    own_h, near_h = activate_early(own_sums, []), activate_early(swap(part, "x"), [v_first])
    far_part = late_far(far, weights + [w_far])
    rest_part = late_rest([first, second, rows], w_far, [far_part])
    far_h = activate_far(swap(far_part, "x"))
    rest = swap(rest_part, "x")
    near_h = activate_rest(rest, near_h, 0, [v_second, v_far])

    far_out = down_far([far_h] + [shift(far_h, "x", d) for d in (1, 2, 3)], v_all, lax.axis_index("x"))
    got = pass_on(far_out, "zhi", 1)
    first_out, second_out = down(swap(near_h, "x"), v_all, (half, wide))
    back = pass_on(first_out, "zhi", -1)
    joined = join(second_out, got)
    ahead = pass_on(joined, "zhi", 1)

    own_h = activate_rest(rest, own_h, 2, [first_out])
    (own_out,) = down(swap(own_h, "x"), v_all, (wide,))
    result = (own_out + ahead.astype(wide) + back.astype(wide)).reshape(2, 64, 1024)

    ids = jnp.arange(4, dtype=jnp.int32)[:, None, None]

    def toward(parity):
        return sum(
            jnp.where((owner[k] == ids) & (side[k] == parity), scales[k] * result[k][None], 0.0)
            for k in range(2)
        )

    got = shift(toward(1 - core).astype(half), "core", 1)
    going = (toward(core) + got.astype(wide)).astype(half)
    return jnp.sum(swap(going, "zlo").astype(wide), axis=0, keepdims=True).astype(half)


def solution(mesh):
    fine = Mesh(mesh.devices.reshape(4, 2, 4, 4, 4), ("zlo", "core", "x", "y", "zhi"))
    seqs, pos = ("zlo", "core"), ("y", "zhi")
    return jax.shard_map(
        on_device,
        mesh=fine,
        in_specs=(
            P(seqs, pos, "x"),
            P(),
            P(),
            P(seqs, "x", None, pos),
            P(seqs, pos, "x"),
        ),
        out_specs=P(seqs, pos, "x"),
        check_vma=False,
    )
```

```python
import jax
import jax.numpy as jnp
from jax import lax
from jax.experimental import pallas as pl
from jax.experimental.pallas import tpu as pltpu
from jax.sharding import Mesh, PartitionSpec as P

wide = jnp.float32
half = jnp.bfloat16
LIMIT = 60 * 2**20
SOME = pl.CostEstimate(flops=10 * 10**9, bytes_accessed=1024, transcendentals=0)
LONG = pl.CostEstimate(flops=10**11, bytes_accessed=1024, transcendentals=0)
COST = pl.CostEstimate(flops=1024, bytes_accessed=1024, transcendentals=0)
ANY = pl.BlockSpec(memory_space=pl.ANY)
WHOLE = pl.BlockSpec(memory_space=pltpu.VMEM)


def shift(a, axis, by):
    n = lax.axis_size(axis)
    return lax.ppermute(a, axis, [(i, (i + by) % n) for i in range(n)])


def pass_on(a, axis, by):
    n = lax.axis_size(axis)
    return lax.ppermute(
        a, ("core", axis), [(c * n + i, c * n + (i + by * (1 - 2 * c)) % n) for c in range(2) for i in range(n)]
    )


def swap(a, axis):
    return lax.all_to_all(a, axis, split_axis=0, concat_axis=0, tiled=True)


DIMS = (((1,), (1,)), ((), ()))


def hold(a, after, cost):
    def kernel(a_ref, *refs):
        refs[-1][...] = a_ref[...]

    return pl.pallas_call(
        kernel,
        in_specs=[WHOLE] + [ANY] * len(after),
        out_specs=WHOLE,
        out_shape=jax.ShapeDtypeStruct(a.shape, a.dtype),
        compiler_params=pltpu.CompilerParams(vmem_limit_bytes=LIMIT),
        cost_estimate=cost,
    )(a, *after)


def fetch(refs, held, sems):
    copies = [pltpu.make_async_copy(ref, held.at[i], sems.at[i]) for i, ref in enumerate(refs)]
    for copy in copies:
        copy.start()
    return copies


def early(pieces, weights, spare, after):
    n = len(pieces)

    def kernel(*refs):
        out_ref, held, sums, sems, out_sems = refs[-5:]
        copies = fetch(refs[n : n + 3], held, sems)
        x = jnp.concatenate([ref[...] for ref in refs[:n]])
        going = []
        for i in range(3):
            copies[i].wait()
            if i == 1 and spare:
                going.append(pltpu.make_async_copy(held.at[1], refs[-6], out_sems.at[3]))
                going[-1].start()
            columns = pl.ds(896 * i, 896)
            out = lax.dot_general(x, held[i], DIMS, preferred_element_type=wide).astype(half)
            for p in range(n):
                sums[:, pl.ds(32 * p, 32), columns] = out[128 * p : 128 * p + 128].reshape(4, 32, 896)
            going.append(pltpu.make_async_copy(sums.at[:, :, columns], out_ref.at[:, :, columns], out_sems.at[i]))
            going[-1].start()
        for copy in going:
            copy.wait()

    shapes = [(896, 1024)] * spare + [(4, 32 * n, 2688)]
    return pl.pallas_call(
        kernel,
        in_specs=[WHOLE] * n + [ANY] * (3 + len(after)),
        out_specs=[ANY] * len(shapes),
        out_shape=[jax.ShapeDtypeStruct(shape, half) for shape in shapes],
        scratch_shapes=[
            pltpu.VMEM((3, 896, 1024), half),
            pltpu.VMEM((4, 32 * n, 2688), half),
            pltpu.SemaphoreType.DMA((3,)),
            pltpu.SemaphoreType.DMA((4,)),
        ],
        compiler_params=pltpu.CompilerParams(vmem_limit_bytes=LIMIT),
        cost_estimate=LONG if spare else SOME,
    )(*pieces, *weights, *after)


def late(pieces, weights):
    def kernel(*refs):
        out_ref, rest_ref, held, sums, rest, sems, out_sems = refs[-7:]
        copies = fetch(refs[4:8], held, sems)
        going = []
        for i in range(4):
            copies[i].wait()
            columns = pl.ds(896 * i, 896)
            out = lax.dot_general(refs[0][...], held[i], DIMS, preferred_element_type=wide).astype(half)
            sums[:, :, columns] = out.reshape(4, 32, 896)
            going.append(pltpu.make_async_copy(sums.at[:, :, columns], out_ref.at[:, :, columns], out_sems.at[i]))
            going[-1].start()
        x = jnp.concatenate([ref[...] for ref in refs[1:4]])
        out = lax.dot_general(x, held[3], DIMS, preferred_element_type=wide).astype(half)
        for p in range(3):
            rest[:, :, pl.ds(896 * p, 896)] = out[128 * p : 128 * p + 128].reshape(4, 32, 896)
        going.append(pltpu.make_async_copy(rest, rest_ref, out_sems.at[4]))
        going[-1].start()
        for copy in going:
            copy.wait()

    return pl.pallas_call(
        kernel,
        in_specs=[WHOLE] * 4 + [ANY] * 4,
        out_specs=[ANY] * 2,
        out_shape=[jax.ShapeDtypeStruct((4, 32, n), half) for n in (3584, 2688)],
        scratch_shapes=[
            pltpu.VMEM((4, 896, 1024), half),
            pltpu.VMEM((4, 32, 3584), half),
            pltpu.VMEM((4, 32, 2688), half),
            pltpu.SemaphoreType.DMA((4,)),
            pltpu.SemaphoreType.DMA((5,)),
        ],
        compiler_params=pltpu.CompilerParams(vmem_limit_bytes=LIMIT),
        cost_estimate=LONG,
    )(*pieces, *weights)


def act(gate, up):
    return (gate / (1.0 + jnp.exp(-gate)) * up).astype(half)


def block(sums, i):
    at = 896 * i
    return act(sums[:, at : at + 448], sums[:, at + 448 : at + 896])


def activate_early(sums, after):
    rows = sums.shape[1]

    def kernel(sums_ref, *refs):
        out_ref = refs[-1]
        total = jnp.sum(sums_ref[...].astype(wide), axis=0)
        out_ref[...] = jnp.concatenate([block(total, i) for i in range(3)], axis=1)

    return pl.pallas_call(
        kernel,
        grid=(1,),
        in_specs=[pl.BlockSpec((4, rows, 2688), lambda i: (0, 0, 0))] + [ANY] * len(after),
        out_specs=pl.BlockSpec((rows, 1344), lambda i: (0, 0)),
        out_shape=jax.ShapeDtypeStruct((rows, 1344), half),
        compiler_params=pltpu.CompilerParams(vmem_limit_bytes=LIMIT),
        cost_estimate=COST,
    )(sums, *after)


def activate_far(sums, after):
    def kernel(sums_ref, after_ref, out_ref):
        total = jnp.sum(sums_ref[...].astype(wide), axis=0)
        out_ref[...] = jnp.concatenate([block(total, i) for i in range(4)], axis=1)

    return pl.pallas_call(
        kernel,
        grid=(1,),
        in_specs=[pl.BlockSpec((4, 32, 3584), lambda i: (0, 0, 0)), ANY],
        out_specs=pl.BlockSpec((32, 1792), lambda i: (0, 0)),
        out_shape=jax.ShapeDtypeStruct((32, 1792), half),
        compiler_params=pltpu.CompilerParams(vmem_limit_bytes=LIMIT),
        cost_estimate=LONG,
    )(sums, after)


def activate_rest(sums, begun, at, after):
    n = begun.shape[0] // 32

    def kernel(sums_ref, begun_ref, *refs):
        total = jnp.sum(sums_ref[:, :, 896 * at : 896 * (at + n)].astype(wide), axis=0)
        blocks = jnp.concatenate([block(total, i) for i in range(n)])
        hidden = jnp.concatenate([begun_ref[...], blocks], axis=1)
        for j in range(4):
            refs[-1][j] = hidden

    return pl.pallas_call(
        kernel,
        grid=(1,),
        in_specs=[
            pl.BlockSpec((4, 32, 2688), lambda i: (0, 0, 0)),
            pl.BlockSpec((32 * n, 1344), lambda i: (0, 0)),
        ]
        + [ANY] * len(after),
        out_specs=pl.BlockSpec((4, 32 * n, 1792), lambda i: (0, 0, 0)),
        out_shape=jax.ShapeDtypeStruct((4, 32 * n, 1792), half),
        compiler_params=pltpu.CompilerParams(vmem_limit_bytes=LIMIT),
        cost_estimate=COST,
    )(sums, begun, *after)


def down(hidden, weights, types):
    n = len(types)

    def kernel(*refs):
        hidden_ref, v_refs, outs = refs[0], refs[1:5], refs[5:]
        v = jnp.concatenate([ref[...] for ref in v_refs])
        for i, out in enumerate(outs):
            rows = hidden_ref[:, pl.ds(32 * i, 32), :].reshape(128, 1792)
            out[...] = jnp.dot(rows, v, preferred_element_type=wide).astype(out.dtype)

    return pl.pallas_call(
        kernel,
        grid=(2,),
        in_specs=[pl.BlockSpec((4, 32 * n, 1792), lambda i: (0, 0, 0))]
        + [pl.BlockSpec((448, 512), lambda i: (0, i))] * 4,
        out_specs=[pl.BlockSpec((128, 512), lambda i: (0, i))] * n,
        out_shape=[jax.ShapeDtypeStruct((128, 1024), t) for t in types],
        compiler_params=pltpu.CompilerParams(vmem_limit_bytes=LIMIT),
        cost_estimate=COST,
    )(hidden, *weights)


def down_far(pieces, weights, x):
    def kernel(x_ref, *refs):
        v_refs, out_ref = refs[4:8], refs[8]
        v = jnp.concatenate([ref[...] for ref in v_refs])
        rows = jnp.concatenate([ref[...] for ref in refs[:4]])
        out = jnp.dot(rows, v, preferred_element_type=wide).astype(half)
        for d in range(4):
            at = pl.multiple_of(((x_ref[0] - d) & 3) * 32, 32)
            out_ref[pl.ds(at, 32), :] = out[32 * d : 32 * d + 32]

    return pl.pallas_call(
        kernel,
        grid=(2,),
        in_specs=[pl.BlockSpec(memory_space=pltpu.SMEM)]
        + [pl.BlockSpec((32, 1792), lambda i: (0, 0))] * 4
        + [pl.BlockSpec((448, 512), lambda i: (0, i))] * 4,
        out_specs=pl.BlockSpec((128, 512), lambda i: (0, i)),
        out_shape=jax.ShapeDtypeStruct((128, 1024), half),
        compiler_params=pltpu.CompilerParams(vmem_limit_bytes=LIMIT),
        cost_estimate=LONG,
    )(x.reshape(1), *pieces, *weights)


def join(a, b):
    def kernel(a_ref, b_ref, out_ref):
        out_ref[...] = (a_ref[...] + b_ref[...].astype(wide)).astype(half)

    return pl.pallas_call(
        kernel,
        in_specs=[WHOLE] * 2,
        out_specs=WHOLE,
        out_shape=jax.ShapeDtypeStruct(a.shape, half),
        compiler_params=pltpu.CompilerParams(vmem_limit_bytes=LIMIT),
        cost_estimate=LONG,
    )(a, b)


def on_device(tokens, routes, route_gates, w_in, w_down):
    core = lax.axis_index("core")
    zlo = lax.axis_index("zlo")
    expert = zlo * 2 + core

    mine = [tokens[0]] + [shift(tokens[0], "zlo", d) for d in (1, 2, 3)]
    w_own, v_own = jnp.transpose(w_in[0], (1, 2, 0)).reshape(896, 1024), w_down[0]
    w_first, w_second = pass_on(w_own, "y", 1), pass_on(w_own, "y", -1)
    weights = [w_own, w_first, w_second]

    matches = routes[:, :, None] == jnp.arange(8, dtype=jnp.int32)[None, None, :]
    hit = jnp.sum(matches.astype(jnp.int32), axis=1)
    slot = jnp.cumsum(hit, axis=0) - hit
    weight = jnp.sum(route_gates[:, :, None] * matches.astype(wide), axis=1)
    names = jnp.arange(8, dtype=jnp.int32)

    def places(e):
        taken = lax.dynamic_index_in_dim(hit, e, 1, keepdims=False)
        place = lax.dynamic_index_in_dim(slot, e, 1, keepdims=False)
        chosen = [(taken == 1) & (place == k) for k in range(2)]
        owner = [jnp.sum(jnp.where(c, names >> 1, 0)) for c in chosen]
        side = [jnp.sum(jnp.where(c, names & 1, 0)) for c in chosen]
        return chosen, owner, side

    chosen, owner, side = places(expert)
    _, owner_too, _ = places(expert + 1 - 2 * core)
    gates = lax.dynamic_index_in_dim(weight, expert, 1, keepdims=False)
    scales = [jnp.sum(jnp.where(c, gates, 0.0)) for c in chosen]

    def taking(owners):
        out = []
        for z in owners:
            away = (zlo - z) & 3
            near = jnp.where(away == 0, mine[0], mine[1])
            out.append(jnp.where(away < 2, near, jnp.where(away == 2, mine[2], mine[3])))
        return out

    other = shift(jnp.concatenate(taking(owner_too)), "core", 1)
    rows = jnp.concatenate(
        [jnp.where(side[k] == core, a, other[64 * k : 64 * k + 64]) for k, a in enumerate(taking(owner))]
    )

    first, second = pass_on(rows, "zhi", 1), pass_on(rows, "zhi", -1)
    w_next, own_part = early([rows], weights, True, [])
    own_sums = swap(own_part, "x")
    w_far = pass_on(w_next, "y", 1)

    (part,) = early([first, second], weights, False, [own_part])
    far = pass_on(hold(first, [own_part], SOME), "zhi", 1)
    v_held = hold(v_own, [own_sums], COST)
    v_first, v_second = pass_on(v_held, "y", 1), pass_on(v_held, "y", -1)
    v_far = pass_on(v_first, "y", 1)
    v_all = [v_own, v_first, v_second, v_far]
    own_h, near_h = activate_early(own_sums, []), activate_early(swap(part, "x"), [v_first])
    far_part, rest_part = late([far, first, second, rows], weights + [w_far])
    far_h = activate_far(swap(far_part, "x"), near_h)
    rest = swap(rest_part, "x")
    near_h = activate_rest(rest, near_h, 0, [v_second, v_far])

    far_out = down_far([far_h] + [shift(far_h, "x", d) for d in (1, 2, 3)], v_all, lax.axis_index("x"))
    got = pass_on(far_out, "zhi", 1)
    first_out, second_out = down(swap(near_h, "x"), v_all, (half, wide))
    back = pass_on(first_out, "zhi", -1)
    joined = join(second_out, got)
    ahead = pass_on(joined, "zhi", 1)

    own_h = activate_rest(rest, own_h, 2, [first_out])
    (own_out,) = down(swap(own_h, "x"), v_all, (wide,))
    result = (own_out + ahead.astype(wide) + back.astype(wide)).reshape(2, 64, 1024)

    ids = jnp.arange(4, dtype=jnp.int32)[:, None, None]

    def toward(parity):
        return sum(
            jnp.where((owner[k] == ids) & (side[k] == parity), scales[k] * result[k][None], 0.0)
            for k in range(2)
        )

    got = shift(toward(1 - core).astype(half), "core", 1)
    going = (toward(core) + got.astype(wide)).astype(half)
    return jnp.sum(swap(going, "zlo").astype(wide), axis=0, keepdims=True).astype(half)


def solution(mesh):
    fine = Mesh(mesh.devices.reshape(4, 2, 4, 4, 4), ("zlo", "core", "x", "y", "zhi"))
    seqs, pos = ("zlo", "core"), ("y", "zhi")
    return jax.shard_map(
        on_device,
        mesh=fine,
        in_specs=(
            P(seqs, pos, "x"),
            P(),
            P(),
            P(seqs, "x", None, pos),
            P(seqs, pos, "x"),
        ),
        out_specs=P(seqs, pos, "x"),
        check_vma=False,
    )
```

```python
import jax
import jax.numpy as jnp
from jax import lax
from jax.experimental import pallas as pl
from jax.experimental.pallas import tpu as pltpu
from jax.sharding import Mesh, PartitionSpec as P

wide = jnp.float32
half = jnp.bfloat16
LIMIT = 60 * 2**20
SOME = pl.CostEstimate(flops=10 * 10**9, bytes_accessed=1024, transcendentals=0)
LONG = pl.CostEstimate(flops=10**11, bytes_accessed=1024, transcendentals=0)
COST = pl.CostEstimate(flops=1024, bytes_accessed=1024, transcendentals=0)
ANY = pl.BlockSpec(memory_space=pl.ANY)
WHOLE = pl.BlockSpec(memory_space=pltpu.VMEM)


def shift(a, axis, by):
    n = lax.axis_size(axis)
    return lax.ppermute(a, axis, [(i, (i + by) % n) for i in range(n)])


def pass_on(a, axis, by):
    n = lax.axis_size(axis)
    return lax.ppermute(
        a, ("core", axis), [(c * n + i, c * n + (i + by * (1 - 2 * c)) % n) for c in range(2) for i in range(n)]
    )


def swap(a, axis):
    return lax.all_to_all(a, axis, split_axis=0, concat_axis=0, tiled=True)


DIMS = (((1,), (1,)), ((), ()))


def hold(a, after, cost):
    def kernel(a_ref, *refs):
        refs[-1][...] = a_ref[...]

    return pl.pallas_call(
        kernel,
        in_specs=[WHOLE] + [ANY] * len(after),
        out_specs=WHOLE,
        out_shape=jax.ShapeDtypeStruct(a.shape, a.dtype),
        compiler_params=pltpu.CompilerParams(vmem_limit_bytes=LIMIT),
        cost_estimate=cost,
    )(a, *after)


def fetch(refs, held, sems):
    copies = [pltpu.make_async_copy(ref, held.at[i], sems.at[i]) for i, ref in enumerate(refs)]
    for copy in copies:
        copy.start()
    return copies


def early(pieces, weights, spare, after):
    n = len(pieces)

    def kernel(*refs):
        out_ref, held, sums, sems, out_sems = refs[-5:]
        copies = fetch(refs[n : n + 3], held, sems)
        x = jnp.concatenate([ref[...] for ref in refs[:n]])
        going = []
        for i in range(3):
            copies[i].wait()
            if i == 1 and spare:
                going.append(pltpu.make_async_copy(held.at[1], refs[-6], out_sems.at[3]))
                going[-1].start()
            columns = pl.ds(896 * i, 896)
            out = lax.dot_general(x, held[i], DIMS, preferred_element_type=wide).astype(half)
            for p in range(n):
                sums[:, pl.ds(32 * p, 32), columns] = out[128 * p : 128 * p + 128].reshape(4, 32, 896)
            going.append(pltpu.make_async_copy(sums.at[:, :, columns], out_ref.at[:, :, columns], out_sems.at[i]))
            going[-1].start()
        for copy in going:
            copy.wait()

    shapes = [(896, 1024)] * spare + [(4, 32 * n, 2688)]
    return pl.pallas_call(
        kernel,
        in_specs=[WHOLE] * n + [ANY] * (3 + len(after)),
        out_specs=[ANY] * len(shapes),
        out_shape=[jax.ShapeDtypeStruct(shape, half) for shape in shapes],
        scratch_shapes=[
            pltpu.VMEM((3, 896, 1024), half),
            pltpu.VMEM((4, 32 * n, 2688), half),
            pltpu.SemaphoreType.DMA((3,)),
            pltpu.SemaphoreType.DMA((4,)),
        ],
        compiler_params=pltpu.CompilerParams(vmem_limit_bytes=LIMIT),
        cost_estimate=LONG if spare else SOME,
    )(*pieces, *weights, *after)


def late(pieces, weights):
    def kernel(*refs):
        out_ref, rest_ref, held, sums, rest, sems, out_sems = refs[-7:]
        copies = fetch(refs[4:8], held, sems)
        going = []
        for i in range(4):
            copies[i].wait()
            columns = pl.ds(896 * i, 896)
            out = lax.dot_general(refs[0][...], held[i], DIMS, preferred_element_type=wide).astype(half)
            sums[:, :, columns] = out.reshape(4, 32, 896)
            going.append(pltpu.make_async_copy(sums.at[:, :, columns], out_ref.at[:, :, columns], out_sems.at[i]))
            going[-1].start()
        x = jnp.concatenate([ref[...] for ref in refs[1:4]])
        out = lax.dot_general(x, held[3], DIMS, preferred_element_type=wide).astype(half)
        for p in range(3):
            rest[:, :, pl.ds(896 * p, 896)] = out[128 * p : 128 * p + 128].reshape(4, 32, 896)
        going.append(pltpu.make_async_copy(rest, rest_ref, out_sems.at[4]))
        going[-1].start()
        for copy in going:
            copy.wait()

    return pl.pallas_call(
        kernel,
        in_specs=[WHOLE] * 4 + [ANY] * 4,
        out_specs=[ANY] * 2,
        out_shape=[jax.ShapeDtypeStruct((4, 32, n), half) for n in (3584, 2688)],
        scratch_shapes=[
            pltpu.VMEM((4, 896, 1024), half),
            pltpu.VMEM((4, 32, 3584), half),
            pltpu.VMEM((4, 32, 2688), half),
            pltpu.SemaphoreType.DMA((4,)),
            pltpu.SemaphoreType.DMA((5,)),
        ],
        compiler_params=pltpu.CompilerParams(vmem_limit_bytes=LIMIT),
        cost_estimate=LONG,
    )(*pieces, *weights)


def act(gate, up):
    return (gate / (1.0 + jnp.exp(-gate)) * up).astype(half)


def block(sums, i):
    at = 896 * i
    return act(sums[:, at : at + 448], sums[:, at + 448 : at + 896])


def activate_early(sums, after):
    rows = sums.shape[1]

    def kernel(sums_ref, *refs):
        out_ref = refs[-1]
        total = jnp.sum(sums_ref[...].astype(wide), axis=0)
        out_ref[...] = jnp.concatenate([block(total, i) for i in range(3)], axis=1)

    return pl.pallas_call(
        kernel,
        grid=(1,),
        in_specs=[pl.BlockSpec((4, rows, 2688), lambda i: (0, 0, 0))] + [ANY] * len(after),
        out_specs=pl.BlockSpec((rows, 1344), lambda i: (0, 0)),
        out_shape=jax.ShapeDtypeStruct((rows, 1344), half),
        compiler_params=pltpu.CompilerParams(vmem_limit_bytes=LIMIT),
        cost_estimate=COST,
    )(sums, *after)


def activate_far(sums, after):
    def kernel(sums_ref, after_ref, out_ref):
        total = jnp.sum(sums_ref[...].astype(wide), axis=0)
        out_ref[...] = jnp.concatenate([block(total, i) for i in range(4)], axis=1)

    return pl.pallas_call(
        kernel,
        grid=(1,),
        in_specs=[pl.BlockSpec((4, 32, 3584), lambda i: (0, 0, 0)), ANY],
        out_specs=pl.BlockSpec((32, 1792), lambda i: (0, 0)),
        out_shape=jax.ShapeDtypeStruct((32, 1792), half),
        compiler_params=pltpu.CompilerParams(vmem_limit_bytes=LIMIT),
        cost_estimate=LONG,
    )(sums, after)


def activate_rest(sums, begun, at, after):
    n = begun.shape[0] // 32

    def kernel(sums_ref, begun_ref, *refs):
        total = jnp.sum(sums_ref[:, :, 896 * at : 896 * (at + n)].astype(wide), axis=0)
        blocks = jnp.concatenate([block(total, i) for i in range(n)])
        hidden = jnp.concatenate([begun_ref[...], blocks], axis=1)
        for j in range(4):
            refs[-1][j] = hidden

    return pl.pallas_call(
        kernel,
        grid=(1,),
        in_specs=[
            pl.BlockSpec((4, 32, 2688), lambda i: (0, 0, 0)),
            pl.BlockSpec((32 * n, 1344), lambda i: (0, 0)),
        ]
        + [ANY] * len(after),
        out_specs=pl.BlockSpec((4, 32 * n, 1792), lambda i: (0, 0, 0)),
        out_shape=jax.ShapeDtypeStruct((4, 32 * n, 1792), half),
        compiler_params=pltpu.CompilerParams(vmem_limit_bytes=LIMIT),
        cost_estimate=COST,
    )(sums, begun, *after)


def times_blocks(rows, blocks):
    return sum(
        jnp.dot(rows[:, 448 * i : 448 * i + 448], ref[...], preferred_element_type=wide)
        for i, ref in enumerate(blocks)
    )


def down(hidden, weights, types):
    n = len(types)

    def kernel(*refs):
        hidden_ref, v_refs, outs = refs[0], refs[1:5], refs[5:]
        rows = jnp.concatenate([hidden_ref[:, pl.ds(32 * i, 32), :].reshape(128, 1792) for i in range(n)])
        sums = times_blocks(rows, v_refs)
        for i, out in enumerate(outs):
            out[...] = sums[128 * i : 128 * i + 128].astype(out.dtype)

    return pl.pallas_call(
        kernel,
        grid=(2,),
        in_specs=[pl.BlockSpec((4, 32 * n, 1792), lambda i: (0, 0, 0))]
        + [pl.BlockSpec((448, 512), lambda i: (0, i))] * 4,
        out_specs=[pl.BlockSpec((128, 512), lambda i: (0, i))] * n,
        out_shape=[jax.ShapeDtypeStruct((128, 1024), t) for t in types],
        compiler_params=pltpu.CompilerParams(vmem_limit_bytes=LIMIT),
        cost_estimate=COST,
    )(hidden, *weights)


def down_far(pieces, weights, x):
    def kernel(x_ref, *refs):
        v_refs, out_ref = refs[4:8], refs[8]
        rows = jnp.concatenate([ref[...] for ref in refs[:4]])
        out = times_blocks(rows, v_refs).astype(half)
        for d in range(4):
            at = pl.multiple_of(((x_ref[0] - d) & 3) * 32, 32)
            out_ref[pl.ds(at, 32), :] = out[32 * d : 32 * d + 32]

    return pl.pallas_call(
        kernel,
        grid=(2,),
        in_specs=[pl.BlockSpec(memory_space=pltpu.SMEM)]
        + [pl.BlockSpec((32, 1792), lambda i: (0, 0))] * 4
        + [pl.BlockSpec((448, 512), lambda i: (0, i))] * 4,
        out_specs=pl.BlockSpec((128, 512), lambda i: (0, i)),
        out_shape=jax.ShapeDtypeStruct((128, 1024), half),
        compiler_params=pltpu.CompilerParams(vmem_limit_bytes=LIMIT),
        cost_estimate=LONG,
    )(x.reshape(1), *pieces, *weights)


def join(a, b):
    def kernel(a_ref, b_ref, out_ref):
        out_ref[...] = (a_ref[...] + b_ref[...].astype(wide)).astype(half)

    return pl.pallas_call(
        kernel,
        in_specs=[WHOLE] * 2,
        out_specs=WHOLE,
        out_shape=jax.ShapeDtypeStruct(a.shape, half),
        compiler_params=pltpu.CompilerParams(vmem_limit_bytes=LIMIT),
        cost_estimate=LONG,
    )(a, b)


def on_device(tokens, routes, route_gates, w_in, w_down):
    core = lax.axis_index("core")
    zlo = lax.axis_index("zlo")
    expert = zlo * 2 + core

    mine = [tokens[0]] + [shift(tokens[0], "zlo", d) for d in (1, 2, 3)]
    w_own, v_own = jnp.transpose(w_in[0], (1, 2, 0)).reshape(896, 1024), w_down[0]
    w_first, w_second = pass_on(w_own, "y", 1), pass_on(w_own, "y", -1)
    weights = [w_own, w_first, w_second]

    matches = routes[:, :, None] == jnp.arange(8, dtype=jnp.int32)[None, None, :]
    hit = jnp.sum(matches.astype(jnp.int32), axis=1)
    slot = jnp.cumsum(hit, axis=0) - hit
    weight = jnp.sum(route_gates[:, :, None] * matches.astype(wide), axis=1)
    names = jnp.arange(8, dtype=jnp.int32)

    def places(e):
        taken = lax.dynamic_index_in_dim(hit, e, 1, keepdims=False)
        place = lax.dynamic_index_in_dim(slot, e, 1, keepdims=False)
        chosen = [(taken == 1) & (place == k) for k in range(2)]
        owner = [jnp.sum(jnp.where(c, names >> 1, 0)) for c in chosen]
        side = [jnp.sum(jnp.where(c, names & 1, 0)) for c in chosen]
        return chosen, owner, side

    chosen, owner, side = places(expert)
    _, owner_too, _ = places(expert + 1 - 2 * core)
    gates = lax.dynamic_index_in_dim(weight, expert, 1, keepdims=False)
    scales = [jnp.sum(jnp.where(c, gates, 0.0)) for c in chosen]

    def taking(owners):
        out = []
        for z in owners:
            away = (zlo - z) & 3
            near = jnp.where(away == 0, mine[0], mine[1])
            out.append(jnp.where(away < 2, near, jnp.where(away == 2, mine[2], mine[3])))
        return out

    other = shift(jnp.concatenate(taking(owner_too)), "core", 1)
    rows = jnp.concatenate(
        [jnp.where(side[k] == core, a, other[64 * k : 64 * k + 64]) for k, a in enumerate(taking(owner))]
    )

    first, second = pass_on(rows, "zhi", 1), pass_on(rows, "zhi", -1)
    w_next, own_part = early([rows], weights, True, [])
    own_sums = swap(own_part, "x")
    w_far = pass_on(w_next, "y", 1)

    (part,) = early([first, second], weights, False, [own_part])
    far = pass_on(hold(first, [own_part], SOME), "zhi", 1)
    v_held = hold(v_own, [own_sums], COST)
    v_first, v_second = pass_on(v_held, "y", 1), pass_on(v_held, "y", -1)
    v_far = pass_on(v_first, "y", 1)
    v_all = [v_own, v_first, v_second, v_far]
    own_h, near_h = activate_early(own_sums, []), activate_early(swap(part, "x"), [v_first])
    far_part, rest_part = late([far, first, second, rows], weights + [w_far])
    far_h = activate_far(swap(far_part, "x"), near_h)
    rest = swap(rest_part, "x")
    near_h = activate_rest(rest, near_h, 0, [v_second, v_far])

    far_out = down_far([far_h] + [shift(far_h, "x", d) for d in (1, 2, 3)], v_all, lax.axis_index("x"))
    got = pass_on(far_out, "zhi", 1)
    first_out, second_out = down(swap(near_h, "x"), v_all, (half, wide))
    back = pass_on(first_out, "zhi", -1)
    joined = join(second_out, got)
    ahead = pass_on(joined, "zhi", 1)

    own_h = activate_rest(rest, own_h, 2, [first_out])
    (own_out,) = down(swap(own_h, "x"), v_all, (wide,))
    result = (own_out + ahead.astype(wide) + back.astype(wide)).reshape(2, 64, 1024)

    ids = jnp.arange(4, dtype=jnp.int32)[:, None, None]

    def toward(parity):
        return sum(
            jnp.where((owner[k] == ids) & (side[k] == parity), scales[k] * result[k][None], 0.0)
            for k in range(2)
        )

    got = shift(toward(1 - core).astype(half), "core", 1)
    going = (toward(core) + got.astype(wide)).astype(half)
    return jnp.sum(swap(going, "zlo").astype(wide), axis=0, keepdims=True).astype(half)


def solution(mesh):
    fine = Mesh(mesh.devices.reshape(4, 2, 4, 4, 4), ("zlo", "core", "x", "y", "zhi"))
    seqs, pos = ("zlo", "core"), ("y", "zhi")
    return jax.shard_map(
        on_device,
        mesh=fine,
        in_specs=(
            P(seqs, pos, "x"),
            P(),
            P(),
            P(seqs, "x", None, pos),
            P(seqs, pos, "x"),
        ),
        out_specs=P(seqs, pos, "x"),
        check_vma=False,
    )
```

```python
import jax
import jax.numpy as jnp
from jax import lax
from jax.experimental import pallas as pl
from jax.experimental.pallas import tpu as pltpu
from jax.sharding import Mesh, PartitionSpec as P

wide = jnp.float32
half = jnp.bfloat16
LIMIT = 60 * 2**20
SOME = pl.CostEstimate(flops=10 * 10**9, bytes_accessed=1024, transcendentals=0)
LONG = pl.CostEstimate(flops=10**11, bytes_accessed=1024, transcendentals=0)
COST = pl.CostEstimate(flops=1024, bytes_accessed=1024, transcendentals=0)
ANY = pl.BlockSpec(memory_space=pl.ANY)
WHOLE = pl.BlockSpec(memory_space=pltpu.VMEM)


def shift(a, axis, by):
    n = lax.axis_size(axis)
    return lax.ppermute(a, axis, [(i, (i + by) % n) for i in range(n)])


def pass_on(a, axis, by):
    n = lax.axis_size(axis)
    return lax.ppermute(
        a, ("core", axis), [(c * n + i, c * n + (i + by * (1 - 2 * c)) % n) for c in range(2) for i in range(n)]
    )


def swap(a, axis):
    return lax.all_to_all(a, axis, split_axis=0, concat_axis=0, tiled=True)


DIMS = (((1,), (1,)), ((), ()))


def hold(a, after, cost):
    def kernel(a_ref, *refs):
        refs[-1][...] = a_ref[...]

    return pl.pallas_call(
        kernel,
        in_specs=[WHOLE] + [ANY] * len(after),
        out_specs=WHOLE,
        out_shape=jax.ShapeDtypeStruct(a.shape, a.dtype),
        compiler_params=pltpu.CompilerParams(vmem_limit_bytes=LIMIT),
        cost_estimate=cost,
    )(a, *after)


def fetch(refs, held, sems):
    copies = [pltpu.make_async_copy(ref, held.at[i], sems.at[i]) for i, ref in enumerate(refs)]
    for copy in copies:
        copy.start()
    return copies


def early(pieces, weights, spare, after):
    n = len(pieces)

    def kernel(*refs):
        out_ref, held, sums, sems, out_sems = refs[-5:]
        copies = fetch(refs[n : n + 3], held, sems)
        x = jnp.concatenate([ref[...] for ref in refs[:n]])
        going = []
        for i in range(3):
            copies[i].wait()
            if i == 1 and spare:
                going.append(pltpu.make_async_copy(held.at[1], refs[-6], out_sems.at[3]))
                going[-1].start()
            columns = pl.ds(896 * i, 896)
            out = lax.dot_general(x, held[i], DIMS, preferred_element_type=wide).astype(half)
            for p in range(n):
                sums[:, pl.ds(32 * p, 32), columns] = out[128 * p : 128 * p + 128].reshape(4, 32, 896)
            going.append(pltpu.make_async_copy(sums.at[:, :, columns], out_ref.at[:, :, columns], out_sems.at[i]))
            going[-1].start()
        for copy in going:
            copy.wait()

    shapes = [(896, 1024)] * spare + [(4, 32 * n, 2688)]
    return pl.pallas_call(
        kernel,
        in_specs=[WHOLE] * n + [ANY] * (3 + len(after)),
        out_specs=[ANY] * len(shapes),
        out_shape=[jax.ShapeDtypeStruct(shape, half) for shape in shapes],
        scratch_shapes=[
            pltpu.VMEM((3, 896, 1024), half),
            pltpu.VMEM((4, 32 * n, 2688), half),
            pltpu.SemaphoreType.DMA((3,)),
            pltpu.SemaphoreType.DMA((4,)),
        ],
        compiler_params=pltpu.CompilerParams(vmem_limit_bytes=LIMIT),
        cost_estimate=LONG if spare else SOME,
    )(*pieces, *weights, *after)


def late(pieces, weights):
    def kernel(*refs):
        out_ref, rest_ref, held, sums, rest, sems, out_sems = refs[-7:]
        copies = fetch(refs[4:8], held, sems)
        going = []
        for i in range(4):
            copies[i].wait()
            columns = pl.ds(896 * i, 896)
            out = lax.dot_general(refs[0][...], held[i], DIMS, preferred_element_type=wide).astype(half)
            sums[:, :, columns] = out.reshape(4, 32, 896)
            going.append(pltpu.make_async_copy(sums.at[:, :, columns], out_ref.at[:, :, columns], out_sems.at[i]))
            going[-1].start()
        x = jnp.concatenate([ref[...] for ref in refs[1:4]])
        out = lax.dot_general(x, held[3], DIMS, preferred_element_type=wide).astype(half)
        for p in range(3):
            rest[:, :, pl.ds(896 * p, 896)] = out[128 * p : 128 * p + 128].reshape(4, 32, 896)
        going.append(pltpu.make_async_copy(rest, rest_ref, out_sems.at[4]))
        going[-1].start()
        for copy in going:
            copy.wait()

    return pl.pallas_call(
        kernel,
        in_specs=[WHOLE] * 4 + [ANY] * 4,
        out_specs=[ANY] * 2,
        out_shape=[jax.ShapeDtypeStruct((4, 32, n), half) for n in (3584, 2688)],
        scratch_shapes=[
            pltpu.VMEM((4, 896, 1024), half),
            pltpu.VMEM((4, 32, 3584), half),
            pltpu.VMEM((4, 32, 2688), half),
            pltpu.SemaphoreType.DMA((4,)),
            pltpu.SemaphoreType.DMA((5,)),
        ],
        compiler_params=pltpu.CompilerParams(vmem_limit_bytes=LIMIT),
        cost_estimate=LONG,
    )(*pieces, *weights)


def act(gate, up):
    return (gate / (1.0 + jnp.exp(-gate)) * up).astype(half)


def block(sums, i):
    at = 896 * i
    return act(sums[:, at : at + 448], sums[:, at + 448 : at + 896])


def activate_early(sums, after):
    rows = sums.shape[1]

    def kernel(sums_ref, *refs):
        out_ref = refs[-1]
        total = jnp.sum(sums_ref[...].astype(wide), axis=0)
        out_ref[...] = jnp.concatenate([block(total, i) for i in range(3)], axis=1)

    return pl.pallas_call(
        kernel,
        grid=(1,),
        in_specs=[pl.BlockSpec((4, rows, 2688), lambda i: (0, 0, 0))] + [ANY] * len(after),
        out_specs=pl.BlockSpec((rows, 1344), lambda i: (0, 0)),
        out_shape=jax.ShapeDtypeStruct((rows, 1344), half),
        compiler_params=pltpu.CompilerParams(vmem_limit_bytes=LIMIT),
        cost_estimate=COST,
    )(sums, *after)


def activate_far(sums, after):
    def kernel(sums_ref, after_ref, out_ref):
        total = jnp.sum(sums_ref[...].astype(wide), axis=0)
        out_ref[...] = jnp.concatenate([block(total, i) for i in range(4)], axis=1)

    return pl.pallas_call(
        kernel,
        grid=(1,),
        in_specs=[pl.BlockSpec((4, 32, 3584), lambda i: (0, 0, 0)), ANY],
        out_specs=pl.BlockSpec((32, 1792), lambda i: (0, 0)),
        out_shape=jax.ShapeDtypeStruct((32, 1792), half),
        compiler_params=pltpu.CompilerParams(vmem_limit_bytes=LIMIT),
        cost_estimate=LONG,
    )(sums, after)


def activate_rest(sums, begun, at, after):
    n = begun.shape[0] // 32

    def kernel(sums_ref, begun_ref, *refs):
        total = jnp.sum(sums_ref[:, :, 896 * at : 896 * (at + n)].astype(wide), axis=0)
        blocks = jnp.concatenate([block(total, i) for i in range(n)])
        hidden = jnp.concatenate([begun_ref[...], blocks], axis=1)
        for j in range(4):
            refs[-1][j] = hidden

    return pl.pallas_call(
        kernel,
        grid=(1,),
        in_specs=[
            pl.BlockSpec((4, 32, 2688), lambda i: (0, 0, 0)),
            pl.BlockSpec((32 * n, 1344), lambda i: (0, 0)),
        ]
        + [ANY] * len(after),
        out_specs=pl.BlockSpec((4, 32 * n, 1792), lambda i: (0, 0, 0)),
        out_shape=jax.ShapeDtypeStruct((4, 32 * n, 1792), half),
        compiler_params=pltpu.CompilerParams(vmem_limit_bytes=LIMIT),
        cost_estimate=COST,
    )(sums, begun, *after)


def down(hidden, weights, types):
    n = len(types)

    def kernel(*refs):
        hidden_ref, v_refs, outs = refs[0], refs[1:5], refs[5:]
        v = jnp.concatenate([ref[...] for ref in v_refs])
        for i, out in enumerate(outs):
            rows = hidden_ref[:, pl.ds(32 * i, 32), :].reshape(128, 1792)
            out[...] = jnp.dot(rows, v, preferred_element_type=wide).astype(out.dtype)

    return pl.pallas_call(
        kernel,
        grid=(2,),
        in_specs=[pl.BlockSpec((4, 32 * n, 1792), lambda i: (0, 0, 0))]
        + [pl.BlockSpec((448, 512), lambda i: (0, i))] * 4,
        out_specs=[pl.BlockSpec((128, 512), lambda i: (0, i))] * n,
        out_shape=[jax.ShapeDtypeStruct((128, 1024), t) for t in types],
        compiler_params=pltpu.CompilerParams(vmem_limit_bytes=LIMIT),
        cost_estimate=COST,
    )(hidden, *weights)


def down_far(pieces, weights, x):
    def kernel(x_ref, *refs):
        v_refs, out_ref = refs[4:8], refs[8]
        v = jnp.concatenate([ref[...] for ref in v_refs])
        rows = jnp.concatenate([ref[...] for ref in refs[:4]])
        out = jnp.dot(rows, v, preferred_element_type=wide).astype(half)
        for d in range(4):
            at = pl.multiple_of(((x_ref[0] - d) & 3) * 32, 32)
            out_ref[pl.ds(at, 32), :] = out[32 * d : 32 * d + 32]

    return pl.pallas_call(
        kernel,
        grid=(2,),
        in_specs=[pl.BlockSpec(memory_space=pltpu.SMEM)]
        + [pl.BlockSpec((32, 1792), lambda i: (0, 0))] * 4
        + [pl.BlockSpec((448, 512), lambda i: (0, i))] * 4,
        out_specs=pl.BlockSpec((128, 512), lambda i: (0, i)),
        out_shape=jax.ShapeDtypeStruct((128, 1024), half),
        compiler_params=pltpu.CompilerParams(vmem_limit_bytes=LIMIT),
        cost_estimate=LONG,
    )(x.reshape(1), *pieces, *weights)


def join(a, b):
    def kernel(a_ref, b_ref, out_ref):
        out_ref[...] = (a_ref[...] + b_ref[...].astype(wide)).astype(half)

    return pl.pallas_call(
        kernel,
        in_specs=[WHOLE] * 2,
        out_specs=WHOLE,
        out_shape=jax.ShapeDtypeStruct(a.shape, half),
        compiler_params=pltpu.CompilerParams(vmem_limit_bytes=LIMIT),
        cost_estimate=LONG,
    )(a, b)


def finish(own, ahead, back, scales, places):
    def kernel(scale_ref, place_ref, own_ref, ahead_ref, back_ref, scaled_ref, theirs_ref):
        sums = own_ref[...] + ahead_ref[...].astype(wide) + back_ref[...].astype(wide)
        slots = [scale_ref[k] * sums[64 * k : 64 * k + 64] for k in range(2)]
        for k in range(2):
            scaled_ref[64 * k : 64 * k + 64, :] = slots[k]
        for z in range(4):
            picked = [jnp.where(place_ref[k] == z, slots[k], 0.0) for k in range(2)]
            theirs_ref[z] = (picked[0] + picked[1]).astype(half)

    scalars = pl.BlockSpec(memory_space=pltpu.SMEM)
    block = pl.BlockSpec((128, 1024), lambda i: (0, 0))
    return pl.pallas_call(
        kernel,
        grid=(1,),
        in_specs=[scalars] * 2 + [block] * 3,
        out_specs=[block, pl.BlockSpec((4, 64, 1024), lambda i: (0, 0, 0))],
        out_shape=[jax.ShapeDtypeStruct((128, 1024), wide), jax.ShapeDtypeStruct((4, 64, 1024), half)],
        compiler_params=pltpu.CompilerParams(vmem_limit_bytes=LIMIT),
        cost_estimate=COST,
    )(scales, places, own, ahead, back)


def on_device(tokens, routes, route_gates, w_in, w_down):
    core = lax.axis_index("core")
    zlo = lax.axis_index("zlo")
    expert = zlo * 2 + core

    mine = [tokens[0]] + [shift(tokens[0], "zlo", d) for d in (1, 2, 3)]
    w_own, v_own = jnp.transpose(w_in[0], (1, 2, 0)).reshape(896, 1024), w_down[0]
    w_first, w_second = pass_on(w_own, "y", 1), pass_on(w_own, "y", -1)
    weights = [w_own, w_first, w_second]

    matches = routes[:, :, None] == jnp.arange(8, dtype=jnp.int32)[None, None, :]
    hit = jnp.sum(matches.astype(jnp.int32), axis=1)
    slot = jnp.cumsum(hit, axis=0) - hit
    weight = jnp.sum(route_gates[:, :, None] * matches.astype(wide), axis=1)
    names = jnp.arange(8, dtype=jnp.int32)

    def places(e):
        taken = lax.dynamic_index_in_dim(hit, e, 1, keepdims=False)
        place = lax.dynamic_index_in_dim(slot, e, 1, keepdims=False)
        chosen = [(taken == 1) & (place == k) for k in range(2)]
        owner = [jnp.sum(jnp.where(c, names >> 1, 0)) for c in chosen]
        side = [jnp.sum(jnp.where(c, names & 1, 0)) for c in chosen]
        return chosen, owner, side

    chosen, owner, side = places(expert)
    _, owner_too, _ = places(expert + 1 - 2 * core)
    gates = lax.dynamic_index_in_dim(weight, expert, 1, keepdims=False)
    scales = [jnp.sum(jnp.where(c, gates, 0.0)) for c in chosen]

    def taking(owners):
        out = []
        for z in owners:
            away = (zlo - z) & 3
            near = jnp.where(away == 0, mine[0], mine[1])
            out.append(jnp.where(away < 2, near, jnp.where(away == 2, mine[2], mine[3])))
        return out

    other = shift(jnp.concatenate(taking(owner_too)), "core", 1)
    rows = jnp.concatenate(
        [jnp.where(side[k] == core, a, other[64 * k : 64 * k + 64]) for k, a in enumerate(taking(owner))]
    )

    first, second = pass_on(rows, "zhi", 1), pass_on(rows, "zhi", -1)
    w_next, own_part = early([rows], weights, True, [])
    own_sums = swap(own_part, "x")
    w_far = pass_on(w_next, "y", 1)

    (part,) = early([first, second], weights, False, [own_part])
    far = pass_on(hold(first, [own_part], SOME), "zhi", 1)
    v_held = hold(v_own, [own_sums], COST)
    v_first, v_second = pass_on(v_held, "y", 1), pass_on(v_held, "y", -1)
    v_far = pass_on(v_first, "y", 1)
    v_all = [v_own, v_first, v_second, v_far]
    own_h, near_h = activate_early(own_sums, []), activate_early(swap(part, "x"), [v_first])
    far_part, rest_part = late([far, first, second, rows], weights + [w_far])
    far_h = activate_far(swap(far_part, "x"), near_h)
    rest = swap(rest_part, "x")
    near_h = activate_rest(rest, near_h, 0, [v_second, v_far])

    far_out = down_far([far_h] + [shift(far_h, "x", d) for d in (1, 2, 3)], v_all, lax.axis_index("x"))
    got = pass_on(far_out, "zhi", 1)
    first_out, second_out = down(swap(near_h, "x"), v_all, (half, wide))
    back = pass_on(first_out, "zhi", -1)
    joined = join(second_out, got)
    ahead = pass_on(joined, "zhi", 1)

    own_h = activate_rest(rest, own_h, 2, [first_out])
    (own_out,) = down(swap(own_h, "x"), v_all, (wide,))
    places = jnp.stack([jnp.where(side[k] == core, -1, owner[k]) for k in range(2)])
    scaled, theirs = finish(own_out, ahead, back, jnp.stack(scales), places)

    got = shift(theirs, "core", 1)
    ids = jnp.arange(4, dtype=jnp.int32)[:, None, None]
    going = got.astype(wide)
    for k in range(2):
        going += jnp.where((owner[k] == ids) & (side[k] == core), scaled[None, 64 * k : 64 * k + 64], 0.0)
    return jnp.sum(swap(going.astype(half), "zlo").astype(wide), axis=0, keepdims=True).astype(half)


def solution(mesh):
    fine = Mesh(mesh.devices.reshape(4, 2, 4, 4, 4), ("zlo", "core", "x", "y", "zhi"))
    seqs, pos = ("zlo", "core"), ("y", "zhi")
    return jax.shard_map(
        on_device,
        mesh=fine,
        in_specs=(
            P(seqs, pos, "x"),
            P(),
            P(),
            P(seqs, "x", None, pos),
            P(seqs, pos, "x"),
        ),
        out_specs=P(seqs, pos, "x"),
        check_vma=False,
    )
```
